512 devices in a mesh: dp: 64 (over y, z_hi, core), space: 8 (over z_lo, x).
Axes of the slice: x: 4, y: 8, z: 8 (z_hi: 4, z_lo: 2; z = z_hi * 2 + z_lo), core: 2. Of those that a mesh axis runs over, the one named last changes fastest.
Arguments:
- expanded: bfloat16 [512, 32, 16, 1152], P('dp', 'space'), may hold values from -6 to 6
- dw_four: float32 [9, 1152], replicated, may hold values from -2 to 2
- squeeze_down: bfloat16 [1152, 86], replicated, may hold values from -0.75 to 0.75
- squeeze_up: bfloat16 [86, 1152], replicated, may hold values from -1.25 to 1.25
- project_four: bfloat16 [1152, 344], replicated, may hold values from -0.1875 to 0.1875
- expand_five: bfloat16 [344, 1152], replicated, may hold values from -0.3125 to 0.3125
- dw_five: float32 [25, 1152], replicated, may hold values from -1.25 to 1.25
- project_five: bfloat16 [1152, 480], replicated, may hold values from -0.1875 to 0.1875
- cotangent: bfloat16 [512, 32, 16, 480], P(('dp', 'space')), may hold values from -6 to 6
Outputs:
- grad_expand: float32 [344, 1152], P(None, 'dp')
- grad_depthwise: float32 [25, 1152], P(None, 'dp')
- grad_project: float32 [1152, 480], P('dp')
- input_cotangent: bfloat16 [512, 32, 16, 344], P('dp', 'space')
The draws below stay inside these ranges and needn't reach their ends.
All inputs are finite; a program needn't handle non-finite values.
Results may differ from the reference program's by a relative error of at most 0.018.
Values may be sent and summed in bfloat16 or wider, within the bound.
A program may use at most 64 MiB of HBM per device.

```python
import math
import jax
import jax.numpy as jnp
from jax import lax

C4 = 344
C5 = 480
EXP = 1152
SQZ = 86
W = 16
H = 32
SAMPLES = 512


def draw_expanded(key, part):
    key = jax.random.fold_in(key, 11)
    shape = (SAMPLES, H, W, EXP)
    row_pos = jnp.arange(H, dtype=jnp.float32)
    ramp = 0.5 + 1.5 * row_pos / max(H - 1, 1)
    values = jax.random.normal(key, shape, jnp.float32)
    values = jnp.clip(values * ramp[None, :, None, None], -6.0, 6.0)
    return values.astype(jnp.bfloat16)


def steps_of(own_key, extent, cuts, smallest, high):
    def one(axis_at, parts):
        steps = jax.random.uniform(jax.random.fold_in(jax.random.fold_in(own_key, 6), axis_at), (parts,), jnp.float32, smallest / len(cuts), high / len(cuts))
        return jnp.repeat(jnp.exp(steps), extent[axis_at] // parts).reshape((-1,) + (1,) * (len(extent) - axis_at - 1))

    level = one(*cuts[0])
    for cut in cuts[1:]:
        level = level * one(*cut)
    return level


def noise(key, shape, deviation, limit, cuts=(), kind=jnp.bfloat16):
    factor_of = steps_of(key, shape, cuts, -0.22, 0.18) if cuts else 1.0
    entries = jax.random.normal(key, shape, jnp.float32) * deviation * factor_of
    return jnp.minimum(jnp.maximum(entries, -limit), limit).astype(kind)


def setup_inputs(seed: int = 0) -> dict:
    splits = jax.random.split(jax.random.key(seed), 10)
    expanded = draw_expanded(jax.random.fold_in(splits[9], 71), 0)
    dw_four = noise(splits[1], (9, EXP), 9 ** -0.5, 2.0, (), jnp.float32)
    squeeze_down = noise(splits[2], (EXP, SQZ), (EXP // 16) ** -0.5, 0.75)
    squeeze_up = noise(splits[3], (SQZ, EXP), (SQZ // 4) ** -0.5, 1.25)
    project_four = noise(splits[4], (EXP, C4), EXP ** -0.5, 0.1875)
    expand_five = noise(splits[5], (C4, EXP), C4 ** -0.5, 0.3125)
    dw_five = noise(splits[6], (25, EXP), 25 ** -0.5, 1.25, (), jnp.float32)
    project_five = noise(splits[7], (EXP, C5), EXP ** -0.5, 0.1875)
    cotangent = noise(splits[8], (SAMPLES, H, W, C5), 1.0, 6.0, ((0, 512),))
    return {"expanded": expanded, "dw_four": dw_four, "squeeze_down": squeeze_down, "squeeze_up": squeeze_up, "project_four": project_four, "expand_five": expand_five, "dw_five": dw_five, "project_five": project_five, "cotangent": cotangent}


def swish_act(value):
    return value * jax.nn.sigmoid(value)

def swish_slope(value):
    sig_value = jax.nn.sigmoid(value)
    return sig_value * (1.0 + value * (1.0 - sig_value))

def depthwise(padded, kernel, span_cells):
    reach_cells = span_cells // 2
    row_count = padded.shape[1] - 2 * reach_cells
    wide_cols = jnp.pad(padded, ((0, 0), (0, 0), (reach_cells, reach_cells), (0, 0)))
    col_count = padded.shape[2]
    summed = jnp.zeros((padded.shape[0], row_count, col_count, padded.shape[3]), jnp.float32)
    for i in range(span_cells):
        for j in range(span_cells):
            window = wide_cols[:, i:i + row_count, j:j + col_count, :].astype(jnp.float32)
            summed = summed + window * kernel[i * span_cells + j]
    return summed

def kernel_grad(padded, grad_field, span_cells):
    reach_cells = span_cells // 2
    row_count = grad_field.shape[1]
    col_count = grad_field.shape[2]
    wide_cols = jnp.pad(padded, ((0, 0), (0, 0), (reach_cells, reach_cells), (0, 0)))
    taps = []
    for i in range(span_cells):
        for j in range(span_cells):
            window = wide_cols[:, i:i + row_count, j:j + col_count, :].astype(jnp.float32)
            taps.append(lax.optimization_barrier(jnp.sum(window * grad_field, axis=(0, 1, 2))))
    return jnp.stack(taps, axis=0)

def finish_four(mixed, image_mean, squeeze_down, squeeze_up, project_four):
    squeezed = swish_act(jnp.dot(image_mean.astype(jnp.bfloat16), squeeze_down, preferred_element_type=jnp.float32)).astype(jnp.bfloat16)
    gate_vals = jax.nn.sigmoid(jnp.dot(squeezed, squeeze_up, preferred_element_type=jnp.float32))
    hidden = (mixed * gate_vals[:, None, None, :]).astype(jnp.bfloat16)
    s, r, w, e = hidden.shape
    return jnp.dot(hidden.reshape(-1, e), project_four, preferred_element_type=jnp.float32).astype(jnp.bfloat16).reshape(s, r, w, -1)

def section_five(inputs, expand_five, dw_five, project_five, cotangent):
    s, h, w, c = inputs.shape
    flat_rows = inputs.reshape(-1, c)
    pre_act = jnp.dot(flat_rows, expand_five, preferred_element_type=jnp.float32)
    chans = pre_act.shape[1]
    spread = swish_act(pre_act).astype(jnp.bfloat16).reshape(s, h, w, chans)
    padded = jnp.pad(spread, ((0, 0), (2, 2), (0, 0), (0, 0)))
    deep_act = depthwise(padded, dw_five, 5)
    hidden = swish_act(deep_act).astype(jnp.bfloat16).reshape(-1, chans)
    cot_rows = cotangent.reshape(-1, cotangent.shape[3])
    grad_project = lax.dot_general(hidden, cot_rows, (((0,), (0,)), ((), ())), preferred_element_type=jnp.float32)
    back_hidden = lax.dot_general(cot_rows, project_five, (((1,), (1,)), ((), ())), preferred_element_type=jnp.float32)
    back_deep = back_hidden.reshape(s, h, w, chans) * swish_slope(deep_act)
    grad_depthwise = kernel_grad(padded, back_deep, 5)
    back_padded = jnp.pad(back_deep, ((0, 0), (2, 2), (0, 0), (0, 0)))
    back_spread = depthwise(back_padded, dw_five[::-1], 5)
    back_pre = (back_spread.reshape(-1, chans) * swish_slope(pre_act)).astype(jnp.bfloat16)
    grad_expand = lax.dot_general(flat_rows, back_pre, (((0,), (0,)), ((), ())), preferred_element_type=jnp.float32)
    back_inputs = lax.dot_general(back_pre, expand_five, (((1,), (1,)), ((), ())), preferred_element_type=jnp.float32)
    return (grad_expand, grad_depthwise, grad_project, back_inputs.astype(jnp.bfloat16).reshape(s, h, w, c))

def reference(expanded, dw_four, squeeze_down, squeeze_up, project_four, expand_five, dw_five, project_five, cotangent):
    factor = 1.0 / math.sqrt(SAMPLES * H * W)

    def one_image(totals_carry, pair):
        image = pair[0][None]
        cot_image = pair[1][None]
        padded = jnp.pad(image, ((0, 0), (1, 1), (0, 0), (0, 0)))
        mixed = swish_act(depthwise(padded, dw_four, 3))
        image_mean = lax.optimization_barrier(jnp.sum(mixed, axis=(1, 2))) / (H * W)
        section_out = finish_four(mixed, image_mean, squeeze_down, squeeze_up, project_four)
        grad_e, grad_d, grad_p, back_inputs = section_five(section_out, expand_five, dw_five, project_five, cot_image)
        return ((totals_carry[0] + grad_e, totals_carry[1] + grad_d, totals_carry[2] + grad_p), back_inputs[0])
    init = (jnp.zeros((C4, EXP), jnp.float32), jnp.zeros((25, EXP), jnp.float32), jnp.zeros((EXP, C5), jnp.float32))
    totals_carry, backs = lax.scan(one_image, init, (expanded, cotangent))
    return (totals_carry[0] * factor, totals_carry[1] * factor, totals_carry[2] * factor, backs)
```

```python
import math

import jax
import jax.numpy as jnp
from jax import lax
from jax.sharding import PartitionSpec as P


def padded_2(block, axis, dim, width):
    count = lax.axis_size(axis)
    forward = [(i, i + 1) for i in range(count - 1)]
    backward = [(target, source) for source, target in forward]
    low = lax.ppermute(
        lax.slice_in_dim(block, block.shape[dim] - width, None, axis=dim), axis, forward
    )
    high = lax.ppermute(lax.slice_in_dim(block, 0, width, axis=dim), axis, backward)
    return jnp.concatenate([low, block, high], axis=dim)


def swish_act(value):
    return value * jax.nn.sigmoid(value)


def swish_slope(value):
    sig_value = jax.nn.sigmoid(value)
    return sig_value * (1.0 + value * (1.0 - sig_value))


def depthwise(padded, kernel, span_cells):
    reach_cells = span_cells // 2
    row_count = padded.shape[1] - 2 * reach_cells
    wide_cols = jnp.pad(padded, ((0, 0), (0, 0), (reach_cells, reach_cells), (0, 0)))
    col_count = padded.shape[2]
    summed = jnp.zeros((padded.shape[0], row_count, col_count, padded.shape[3]), jnp.float32)
    for i in range(span_cells):
        for j in range(span_cells):
            window = wide_cols[:, i : i + row_count, j : j + col_count, :].astype(jnp.float32)
            summed = summed + window * kernel[i * span_cells + j]
    return summed


def kernel_grad(padded, grad_field, span_cells):
    reach_cells = span_cells // 2
    row_count = grad_field.shape[1]
    col_count = grad_field.shape[2]
    wide_cols = jnp.pad(padded, ((0, 0), (0, 0), (reach_cells, reach_cells), (0, 0)))
    taps = []
    for i in range(span_cells):
        for j in range(span_cells):
            window = wide_cols[:, i : i + row_count, j : j + col_count, :].astype(jnp.float32)
            taps.append(jnp.sum(window * grad_field, axis=(0, 1, 2)))
    return jnp.stack(taps, axis=0)


def finish_four(mixed, sums, cell_count, squeeze_down, squeeze_up, project_four):
    group = lax.axis_size("space")
    part = jnp.dot(sums / cell_count, squeeze_down.astype(jnp.float32), precision="highest")
    part = jnp.pad(part, ((0, 0), (0, -part.shape[1] % 128)))
    parts = lax.all_to_all(
        jnp.broadcast_to(part, (group,) + part.shape), "space", split_axis=0, concat_axis=0
    )
    total = jnp.sum(parts, axis=0)[:, : squeeze_down.shape[1]]
    squeezed = swish_act(total).astype(jnp.bfloat16)
    gate_vals = jax.nn.sigmoid(jnp.dot(squeezed, squeeze_up, preferred_element_type=jnp.float32))
    hidden = (mixed * gate_vals[:, None, None, :]).astype(jnp.bfloat16)
    s, r, w, e = hidden.shape
    return (
        jnp.dot(hidden.reshape(-1, e), project_four, preferred_element_type=jnp.float32)
        .astype(jnp.bfloat16)
        .reshape(s, r, w, -1)
    )


def section_five(inputs, expand_five, dw_five, project_five, cotangent, factor):
    s, h, w, c = inputs.shape
    flat_rows = inputs.reshape(-1, c)
    pre_act = jnp.dot(flat_rows, expand_five, preferred_element_type=jnp.float32)
    chans = pre_act.shape[1]
    spread = swish_act(pre_act).astype(jnp.bfloat16).reshape(s, h, w, chans)
    padded = jnp.pad(spread, ((0, 0), (2, 2), (0, 0), (0, 0)))
    deep_act = depthwise(padded, dw_five, 5)
    hidden = swish_act(deep_act).astype(jnp.bfloat16).reshape(-1, chans)
    cot_rows = cotangent.reshape(-1, cotangent.shape[3])
    grad_project = lax.dot_general(
        hidden, cot_rows, (((0,), (0,)), ((), ())), preferred_element_type=jnp.float32
    )
    back_hidden = lax.dot_general(
        cot_rows, project_five, (((1,), (1,)), ((), ())), preferred_element_type=jnp.float32
    )
    back_deep = back_hidden.reshape(s, h, w, chans) * swish_slope(deep_act)
    grad_depthwise = kernel_grad(padded, back_deep, 5)
    back_padded = jnp.pad(back_deep, ((0, 0), (2, 2), (0, 0), (0, 0)))
    back_spread = depthwise(back_padded, dw_five[::-1], 5)
    back_pre = (back_spread.reshape(-1, chans) * swish_slope(pre_act)).astype(jnp.bfloat16)
    grad_expand = lax.dot_general(
        back_pre, flat_rows, (((0,), (0,)), ((), ())), preferred_element_type=jnp.float32
    )
    back_inputs = lax.dot_general(
        back_pre, expand_five, (((1,), (1,)), ((), ())), preferred_element_type=jnp.float32
    )
    back_inputs = back_inputs.astype(jnp.bfloat16).reshape(s, h, w, c)
    grads = jnp.concatenate([grad_project, grad_expand, grad_depthwise.T], axis=1) * factor
    return grads, back_inputs


def reduced(grads, width):
    group, shards = lax.axis_size("space"), lax.axis_size("dp")
    rows = grads.shape[0]
    padded = jnp.pad(grads.astype(jnp.bfloat16), ((0, 0), (0, width - grads.shape[1])))
    padded = padded.reshape(rows, group, width // group).transpose(1, 0, 2)
    parts = lax.all_to_all(padded, "space", split_axis=0, concat_axis=0)
    mine = jnp.sum(parts.astype(jnp.float32), axis=0)
    mine = mine.reshape(shards, rows // shards, width // group)
    parts = lax.all_to_all(mine, "dp", split_axis=0, concat_axis=0)
    total = jnp.sum(parts, axis=0)
    wide = lax.all_to_all(
        jnp.broadcast_to(total, (group,) + total.shape), "space", split_axis=0, concat_axis=0
    )
    return wide.transpose(1, 0, 2).reshape(rows // shards, width)


def local(
    expanded,
    dw_four,
    squeeze_down,
    squeeze_up,
    project_four,
    expand_five,
    dw_five,
    project_five,
    cotangent,
):
    group_size = lax.axis_size("space")
    full_rows = expanded.shape[1] * group_size
    cell_count = full_rows * expanded.shape[2]
    padded = padded_2(expanded, "space", 1, 1)
    mixed = swish_act(depthwise(padded, dw_four, 3))
    sums = jnp.sum(mixed, axis=(1, 2))
    row_out = finish_four(mixed, sums, cell_count, squeeze_down, squeeze_up, project_four)
    section_out = lax.all_to_all(row_out, "space", split_axis=0, concat_axis=1, tiled=True)
    total_pixels = (
        cotangent.shape[0] * group_size * lax.axis_size("dp") * full_rows * expanded.shape[2]
    )
    factor = 1.0 / math.sqrt(total_pixels)
    grads, back_inputs = section_five(
        section_out, expand_five, dw_five, project_five, cotangent, factor
    )
    input_cotangent = lax.all_to_all(back_inputs, "space", split_axis=1, concat_axis=0, tiled=True)
    total = reduced(grads, 1024)
    c5, c4 = cotangent.shape[3], expand_five.shape[0]
    taps = dw_five.shape[0]
    grad_p = total[:, :c5]
    grad_e = total[:, c5 : c5 + c4].T
    grad_d = total[:, c5 + c4 : c5 + c4 + taps].T
    return (grad_e, grad_d, grad_p, input_cotangent)


def solution(mesh):
    in_specs = (
        P("dp", "space", None, None),
        P(),
        P(),
        P(),
        P(),
        P(),
        P(),
        P(),
        P(("dp", "space"), None, None, None),
    )
    out_specs = (P(None, "dp"), P(None, "dp"), P("dp", None), P("dp", "space", None, None))
    return jax.shard_map(local, mesh=mesh, in_specs=in_specs, out_specs=out_specs, check_vma=False)
```

```python
import functools
import math

import jax
import jax.numpy as jnp
import numpy as np
from jax import lax
from jax.experimental import pallas as pl
from jax.experimental.pallas import tpu as pltpu
from jax.sharding import PartitionSpec as P

H, W, LANES, RB = 32, 16, 128, 4
TAPS = 5
Y, Z, CORES, KEEP = 8, 4, 2, 2
GROUP = 8
SEGS = 7
DW_AT = 88
F32, BF16 = jnp.float32, jnp.bfloat16
MESH = pl.DeviceIdType.MESH


def padded_2(block, axis, dim, width):
    count = lax.axis_size(axis)
    forward = [(i, i + 1) for i in range(count - 1)]
    backward = [(target, source) for source, target in forward]
    low = lax.ppermute(
        lax.slice_in_dim(block, block.shape[dim] - width, None, axis=dim), axis, forward
    )
    high = lax.ppermute(lax.slice_in_dim(block, 0, width, axis=dim), axis, backward)
    return jnp.concatenate([low, block, high], axis=dim)


def sigmoid(value):
    return 0.5 * jnp.tanh(0.5 * value) + 0.5


def swish_act(value):
    return value * sigmoid(value)


def depthwise(padded, kernel, span_cells):
    reach_cells = span_cells // 2
    row_count = padded.shape[1] - 2 * reach_cells
    wide_cols = jnp.pad(padded, ((0, 0), (0, 0), (reach_cells, reach_cells), (0, 0)))
    col_count = padded.shape[2]
    summed = jnp.zeros((padded.shape[0], row_count, col_count, padded.shape[3]), jnp.float32)
    for i in range(span_cells):
        for j in range(span_cells):
            window = wide_cols[:, i : i + row_count, j : j + col_count, :].astype(jnp.float32)
            summed = summed + window * kernel[i * span_cells + j]
    return summed


def finish_four(mixed, sums, cell_count, squeeze_down, squeeze_up, project_four):
    group = lax.axis_size("space")
    part = jnp.dot(sums / cell_count, squeeze_down.astype(jnp.float32), precision="highest")
    part = jnp.pad(part, ((0, 0), (0, -part.shape[1] % 128)))
    parts = lax.all_to_all(
        jnp.broadcast_to(part, (group,) + part.shape), "space", split_axis=0, concat_axis=0
    )
    total = jnp.sum(parts, axis=0)[:, : squeeze_down.shape[1]]
    squeezed = swish_act(total).astype(jnp.bfloat16)
    gate_vals = jax.nn.sigmoid(jnp.dot(squeezed, squeeze_up, preferred_element_type=jnp.float32))
    hidden = (mixed * gate_vals[:, None, None, :]).astype(jnp.bfloat16)
    s, r, w, e = hidden.shape
    return (
        jnp.dot(hidden.reshape(-1, e), project_four, preferred_element_type=jnp.float32)
        .astype(jnp.bfloat16)
        .reshape(s, r, w, -1)
    )


def shifted(block, step):
    if step == 0:
        return block
    low, high = block[:, :8], block[:, 8:]
    at = lax.broadcasted_iota(jnp.int32, low.shape, 1)
    low_r = pltpu.roll(low, (-step) % 8, 1)
    high_r = pltpu.roll(high, (-step) % 8, 1)
    if step > 0:
        inside = at < 8 - step
        return jnp.concatenate(
            [jnp.where(inside, low_r, high_r), jnp.where(inside, high_r, 0.0)], axis=1
        )
    inside = at >= -step
    return jnp.concatenate(
        [jnp.where(inside, low_r, 0.0), jnp.where(inside, high_r, low_r)], axis=1
    )


def tile_forward(taps, spread, back_hidden, hidden, back_deep):
    def rows(at, carry):
        r = at * RB
        window = spread[pl.ds(r, RB + 4)]
        total = None
        for j in range(TAPS):
            part = None
            for i in range(TAPS):
                term = window[i : i + RB] * taps[i * TAPS + j]
                part = term if part is None else part + term
            part = shifted(part, j - 2)
            total = part if total is None else total + part
        sig = sigmoid(total)
        swish = total * sig
        hidden[pl.ds(r, RB)] = swish.astype(BF16)
        slope = sig + swish * (1.0 - sig)
        back_deep[pl.ds(r + 2, RB)] = back_hidden[pl.ds(r, RB)] * slope
        return carry

    lax.fori_loop(0, H // RB, rows, 0)


def tile_backward(taps, spread, back_deep, pre, back_pre, grad_taps):
    grad_taps[...] = jnp.zeros_like(grad_taps)

    def rows(at, carry):
        r = at * RB
        window = back_deep[pl.ds(r, RB + 4)]
        mine = spread[pl.ds(r + 2, RB)]
        total = None
        for j in range(TAPS):
            moved = shifted(mine, j - 2)
            part = None
            for i in range(TAPS):
                rows_i = window[TAPS - 1 - i : TAPS - 1 - i + RB]
                term = rows_i * taps[i * TAPS + j]
                part = term if part is None else part + term
                prod = rows_i * moved
                prod = prod[:, :8] + prod[:, 8:]
                prod = (prod[0] + prod[1]) + (prod[2] + prod[3])
                grad_taps[i * TAPS + j] += prod
            part = shifted(part, 2 - j)
            total = part if total is None else total + part
        value = pre[pl.ds(r, RB)]
        sig = sigmoid(value)
        slope = sig + value * sig * (1.0 - sig)
        back_pre[pl.ds(r, RB)] = (total * slope).astype(BF16)
        return carry

    lax.fori_loop(0, H // RB, rows, 0)


def five_kernel(
    s_ref, cot_ref, exp_ref, dw_ref, proj_ref, g_ref, back_ref,
    s_pad, cot_pad, pre, spread, bhid, hid, bdeep, bpre, gtaps, gsq, total,
):
    tiles = exp_ref.shape[1] // LANES
    s_pad[...] = jnp.zeros_like(s_pad)
    cot_pad[...] = jnp.zeros_like(cot_pad)
    s_pad[:, : s_ref.shape[1]] = s_ref[...]
    cot_pad[:, : cot_ref.shape[1]] = cot_ref[...]
    spread[...] = jnp.zeros_like(spread)
    bdeep[...] = jnp.zeros_like(bdeep)
    gsq[...] = jnp.zeros_like(gsq)
    total[...] = jnp.zeros_like(total)
    g_ref[GROUP - 1, GROUP - 1] = jnp.zeros((LANES, LANES), BF16)

    def put(t, q, block):
        b = t * SEGS + q
        g_ref[lax.rem(b, GROUP), lax.div(b, GROUP)] = block.astype(BF16)

    def tile(t, carry):
        lanes = pl.ds(pl.multiple_of(t * LANES, LANES), LANES)
        exp = exp_ref[:, lanes]
        pre_v = jnp.dot(s_pad[...], exp, preferred_element_type=F32)
        pre[...] = pre_v.reshape(H, W, LANES)
        spread[2 : 2 + H] = (
            (pre_v * sigmoid(pre_v)).astype(BF16).astype(F32).reshape(H, W, LANES)
        )
        bh = lax.dot_general(
            cot_pad[...], proj_ref[lanes], (((1,), (1,)), ((), ())), preferred_element_type=F32
        )
        bhid[...] = bh.reshape(H, W, LANES)
        taps = [dw_ref[k : k + 1, lanes].reshape(1, 1, LANES) for k in range(TAPS * TAPS)]
        tile_forward(taps, spread, bhid, hid, bdeep)
        gp = lax.dot_general(
            hid[...].reshape(H * W, LANES), cot_pad[...], (((0,), (0,)), ((), ())),
            preferred_element_type=F32,
        )
        for q in range(4):
            put(t, q, gp[:, q * LANES : (q + 1) * LANES])
        tile_backward(taps, spread, bdeep, pre, bpre, gtaps)
        bp = bpre[...].reshape(H * W, LANES)
        ge = lax.dot_general(
            bp, s_pad[...], (((0,), (0,)), ((), ())), preferred_element_type=F32
        )
        gsq[DW_AT : DW_AT + TAPS * TAPS] = jnp.sum(gtaps[...], axis=1)
        put(t, 4, ge[:, :LANES])
        put(t, 5, ge[:, LANES : 2 * LANES])
        put(t, 6, ge[:, 2 * LANES :] + gsq[...].T)
        total[...] += lax.dot_general(
            bp, exp, (((1,), (1,)), ((), ())), preferred_element_type=F32
        )
        return carry

    lax.fori_loop(0, tiles, tile, 0)
    back_ref[...] = total[...].astype(BF16)


def five(section_out, cot, expand, taps, project):
    pixels, wide4, wide5 = H * W, 3 * LANES, 4 * LANES
    vm = pl.BlockSpec(memory_space=pltpu.VMEM)
    return pl.pallas_call(
        five_kernel,
        out_shape=(
            jax.ShapeDtypeStruct((GROUP, GROUP, LANES, LANES), BF16),
            jax.ShapeDtypeStruct((pixels, wide4), BF16),
        ),
        in_specs=[vm] * 5,
        out_specs=(vm, vm),
        scratch_shapes=[
            pltpu.VMEM((pixels, wide4), BF16),
            pltpu.VMEM((pixels, wide5), BF16),
            pltpu.VMEM((H, W, LANES), F32),
            pltpu.VMEM((H + 4, W, LANES), F32),
            pltpu.VMEM((H, W, LANES), F32),
            pltpu.VMEM((H, W, LANES), BF16),
            pltpu.VMEM((H + 4, W, LANES), F32),
            pltpu.VMEM((H, W, LANES), BF16),
            pltpu.VMEM((TAPS * TAPS, 8, LANES), F32),
            pltpu.VMEM((LANES, LANES), F32),
            pltpu.VMEM((pixels, wide4), F32),
        ],
        compiler_params=pltpu.CompilerParams(vmem_limit_bytes=48 * 1024 * 1024),
        cost_estimate=pl.CostEstimate(
            flops=3_000_000_000, bytes_accessed=8_000_000, transcendentals=1_800_000
        ),
    )(section_out, cot, expand, taps, project)


def exchange(source, landed, send, recv, me, peer, device):
    copy = pltpu.make_async_remote_copy(
        src_ref=source,
        dst_ref=landed.at[me],
        send_sem=send.at[peer],
        recv_sem=recv.at[me],
        device_id=device,
        device_id_type=MESH,
    )
    copy.start()
    return copy


def arrived(source, landed, send, recv, peer, device):
    pltpu.make_async_remote_copy(
        src_ref=source,
        dst_ref=landed.at[peer],
        send_sem=send.at[peer],
        recv_sem=recv.at[peer],
        device_id=device,
        device_id_type=MESH,
    ).wait_recv()


def reduce_kernel(
    scale, g_ref, back_ref, out_ref, cots_ref,
    got1, got2, got3, got4, half, send2, send3, own4, pick,
    s1, r1, s2, r2, s3, r3, s4, r4, s5, r5, s6, r6, local_sem,
):
    dp, sp = lax.axis_index("dp"), lax.axis_index("space")
    core = lax.rem(dp, CORES)
    z = lax.rem(lax.div(dp, CORES), Z)
    y = lax.div(dp, CORES * Z)

    def at_space(other):
        return (dp, other)

    def at_core(other):
        return (dp + other - core, sp)

    def at_z(other):
        return (dp + (other - z) * CORES, sp)

    def at_y(other):
        return (dp + (other - y) * (CORES * Z), sp)

    spaces = [lax.rem(sp + step, GROUP) for step in range(1, GROUP)]
    ys = [lax.rem(y + step, Y) for step in range(1, Y)]
    zs = [lax.rem(z + step, Z) for step in range(1, Z)]
    other = 1 - core

    barrier = pltpu.get_barrier_semaphore()
    everyone = (
        [at_space(p) for p in spaces] + [at_core(other)] + [at_y(p) for p in ys] + [at_z(p) for p in zs]
    )
    for device in everyone:
        pl.semaphore_signal(barrier, inc=1, device_id=device, device_id_type=MESH)
    pl.semaphore_wait(barrier, len(everyone))

    sent = [exchange(g_ref.at[p], got1, s1, r1, sp, p, at_space(p)) for p in spaces]
    rows = back_ref.shape[0] // GROUP
    sent += [
        exchange(back_ref.at[pl.ds(pl.multiple_of(p * rows, rows), rows)], cots_ref, s6, r6, sp, p, at_space(p))
        for p in spaces
    ]
    own = pltpu.make_async_copy(
        back_ref.at[pl.ds(pl.multiple_of(sp * rows, rows), rows)], cots_ref.at[sp], local_sem
    )
    own.start()
    for p in spaces:
        arrived(g_ref.at[p], got1, s1, r1, p, at_space(p))
    hold = LANES // CORES
    for b in range(GROUP):
        total = g_ref[sp, b].astype(F32)
        for p in spaces:
            total += got1[p, b].astype(F32)
        half[0, b] = total[:hold]
        half[1, b] = total[hold:]

    sent.append(exchange(half.at[other], got2, s2, r2, core, other, at_core(other)))
    arrived(half.at[other], got2, s2, r2, other, at_core(other))
    for p in range(Y):
        for b in range(GROUP // 2):
            mine = [
                half[core, 2 * b + e, 8 * p : 8 * p + 8] + got2[other, 2 * b + e, 8 * p : 8 * p + 8]
                for e in range(2)
            ]
            send3[p, b] = jnp.concatenate(mine, axis=0).astype(BF16)

    sent += [exchange(send3.at[p], got3, s3, r3, y, p, at_y(p)) for p in ys]
    for p in ys:
        arrived(send3.at[p], got3, s3, r3, p, at_y(p))
    total = send3[y].astype(F32)
    for p in ys:
        total += got3[p].astype(F32)
    own4[...] = total

    sent += [exchange(own4, got4, s4, r4, z, p, at_z(p)) for p in zs]
    for p in zs:
        arrived(own4, got4, s4, r4, p, at_z(p))
    for p in zs:
        total += got4[p]
    total = (total * scale).reshape(GROUP, 8, LANES)
    mine = total[:, :KEEP]
    for p in range(1, Z):
        mine = jnp.where(z == p, total[:, KEEP * p : KEEP * (p + 1)], mine)
    for b in range(GROUP):
        pick[KEEP * b : KEEP * (b + 1)] = mine[b]

    out_ref[sp] = pick[...]
    sent += [exchange(pick, out_ref, s5, r5, sp, p, at_space(p)) for p in spaces]
    for p in spaces:
        arrived(pick, out_ref, s5, r5, p, at_space(p))
    for p in spaces:
        arrived(back_ref.at[pl.ds(0, rows)], cots_ref, s6, r6, p, at_space(p))
    own.wait()
    for copy in sent:
        copy.wait_send()


def reduced(grads, back, scale):
    vm = pl.BlockSpec(memory_space=pltpu.VMEM)
    dma = pltpu.SemaphoreType.DMA
    sems = [dma((n,)) for n in (GROUP, GROUP, CORES, CORES, Y, Y, Z, Z, GROUP, GROUP, GROUP, GROUP)]
    pixels, wide = back.shape
    return pl.pallas_call(
        functools.partial(reduce_kernel, scale),
        out_shape=(
            jax.ShapeDtypeStruct((GROUP, GROUP * KEEP, LANES), F32),
            jax.ShapeDtypeStruct((GROUP, pixels // GROUP, wide), BF16),
        ),
        in_specs=[vm, vm],
        out_specs=(vm, vm),
        scratch_shapes=[
            pltpu.VMEM((GROUP, GROUP, LANES, LANES), BF16),
            pltpu.VMEM((CORES, GROUP, LANES // CORES, LANES), F32),
            pltpu.VMEM((Y, GROUP // 2, 16, LANES), BF16),
            pltpu.VMEM((Z, GROUP // 2, 16, LANES), F32),
            pltpu.VMEM((CORES, GROUP, LANES // CORES, LANES), F32),
            pltpu.VMEM((CORES, 8, LANES), F32),
            pltpu.VMEM((Y, GROUP // 2, 16, LANES), BF16),
            pltpu.VMEM((GROUP // 2, 16, LANES), F32),
            pltpu.VMEM((GROUP * KEEP, LANES), F32),
            *sems,
            dma(()),
        ],
        compiler_params=pltpu.CompilerParams(
            collective_id=0, has_side_effects=True, vmem_limit_bytes=48 * 1024 * 1024
        ),
    )(grads, back)


def channel_order(channels):
    shards = Y * Z * CORES
    each = channels // shards
    order = np.arange(channels).reshape(Y, Z, CORES, each // KEEP, KEEP)
    return order.transpose(3, 2, 0, 1, 4).reshape(-1)


def local(
    expanded,
    dw_four,
    squeeze_down,
    squeeze_up,
    project_four,
    expand_five,
    dw_five,
    project_five,
    cotangent,
):
    group_size = lax.axis_size("space")
    full_rows = expanded.shape[1] * group_size
    cell_count = full_rows * expanded.shape[2]
    c4, channels = expand_five.shape
    c5 = cotangent.shape[3]
    place = (
        lax.broadcasted_iota(jnp.int32, (channels, channels), 0)
        == jnp.asarray(channel_order(channels), jnp.int32)[None, :]
    )
    expand = jnp.dot(
        jnp.pad(expand_five, ((0, 3 * LANES - c4), (0, 0))), place.astype(BF16)
    )
    project = lax.dot_general(
        place.astype(BF16), jnp.pad(project_five, ((0, 0), (0, 4 * LANES - c5))), (((0,), (0,)), ((), ()))
    )
    taps = jnp.dot(dw_five, place.astype(F32), precision="highest")

    padded = padded_2(expanded, "space", 1, 1)
    mixed = swish_act(depthwise(padded, dw_four, 3))
    sums = jnp.sum(mixed, axis=(1, 2))
    row_out = finish_four(mixed, sums, cell_count, squeeze_down, squeeze_up, project_four)
    section_out = lax.all_to_all(row_out, "space", split_axis=0, concat_axis=1, tiled=True)
    total_pixels = (
        cotangent.shape[0] * group_size * lax.axis_size("dp") * full_rows * expanded.shape[2]
    )
    factor = 1.0 / math.sqrt(total_pixels)
    grads, back = five(
        section_out.reshape(H * W, c4), cotangent.reshape(H * W, c5), expand, taps, project
    )
    total, cots = reduced(grads, back, factor)
    input_cotangent = cots[:, :, :c4].reshape(group_size, expanded.shape[1], W, c4)
    tiles = channels // LANES
    total = total.reshape(GROUP, GROUP, KEEP, LANES).transpose(1, 0, 2, 3)
    total = total.reshape(GROUP * GROUP, KEEP, LANES)[: tiles * SEGS]
    total = total.reshape(tiles, SEGS, KEEP, LANES).transpose(0, 2, 1, 3)
    total = total.reshape(tiles * KEEP, SEGS * LANES)
    grad_p = total[:, :c5]
    grad_e = total[:, 4 * LANES : 4 * LANES + c4].T
    grad_d = total[:, 6 * LANES + DW_AT : 6 * LANES + DW_AT + TAPS * TAPS].T
    return (grad_e, grad_d, grad_p, input_cotangent)


def solution(mesh):
    in_specs = (
        P("dp", "space", None, None),
        P(),
        P(),
        P(),
        P(),
        P(),
        P(),
        P(),
        P(("dp", "space"), None, None, None),
    )
    out_specs = (P(None, "dp"), P(None, "dp"), P("dp", None), P("dp", "space", None, None))
    return jax.shard_map(local, mesh=mesh, in_specs=in_specs, out_specs=out_specs, check_vma=False)
```

```python
import functools
import math

import jax
import jax.numpy as jnp
import numpy as np
from jax import lax
from jax.experimental import pallas as pl
from jax.experimental.pallas import tpu as pltpu
from jax.sharding import PartitionSpec as P

H, W, LANES, RB = 32, 16, 128, 4
TAPS = 5
Y, Z, CORES, KEEP = 8, 4, 2, 2
GROUP = 8
SEGS = 7
DW_AT = 88
F32, BF16 = jnp.float32, jnp.bfloat16
MESH = pl.DeviceIdType.MESH


def padded_2(block, axis, dim, width):
    count = lax.axis_size(axis)
    forward = [(i, i + 1) for i in range(count - 1)]
    backward = [(target, source) for source, target in forward]
    low = lax.ppermute(
        lax.slice_in_dim(block, block.shape[dim] - width, None, axis=dim), axis, forward
    )
    high = lax.ppermute(lax.slice_in_dim(block, 0, width, axis=dim), axis, backward)
    return jnp.concatenate([low, block, high], axis=dim)


def sigmoid(value):
    return 0.5 * jnp.tanh(0.5 * value) + 0.5


def swish_act(value):
    return value * sigmoid(value)


def depthwise(padded, kernel, span_cells):
    reach_cells = span_cells // 2
    row_count = padded.shape[1] - 2 * reach_cells
    wide_cols = jnp.pad(padded, ((0, 0), (0, 0), (reach_cells, reach_cells), (0, 0)))
    col_count = padded.shape[2]
    summed = jnp.zeros((padded.shape[0], row_count, col_count, padded.shape[3]), jnp.float32)
    for i in range(span_cells):
        for j in range(span_cells):
            window = wide_cols[:, i : i + row_count, j : j + col_count, :].astype(jnp.float32)
            summed = summed + window * kernel[i * span_cells + j]
    return summed


def finish_four(mixed, sums, cell_count, squeeze_down, squeeze_up, project_four):
    group = lax.axis_size("space")
    part = jnp.dot(sums / cell_count, squeeze_down.astype(jnp.float32), precision="highest")
    part = jnp.pad(part, ((0, 0), (0, -part.shape[1] % 128)))
    parts = lax.all_to_all(
        jnp.broadcast_to(part, (group,) + part.shape), "space", split_axis=0, concat_axis=0
    )
    total = jnp.sum(parts, axis=0)[:, : squeeze_down.shape[1]]
    squeezed = swish_act(total).astype(jnp.bfloat16)
    gate_vals = jax.nn.sigmoid(jnp.dot(squeezed, squeeze_up, preferred_element_type=jnp.float32))
    hidden = (mixed * gate_vals[:, None, None, :]).astype(jnp.bfloat16)
    s, r, w, e = hidden.shape
    return (
        jnp.dot(hidden.reshape(-1, e), project_four, preferred_element_type=jnp.float32)
        .astype(jnp.bfloat16)
        .reshape(s, r, w, -1)
    )


def shifted(block, step):
    if step == 0:
        return block
    low, high = block[:, :8], block[:, 8:]
    at = lax.broadcasted_iota(jnp.int32, low.shape, 1)
    low_r = pltpu.roll(low, (-step) % 8, 1)
    high_r = pltpu.roll(high, (-step) % 8, 1)
    if step > 0:
        inside = at < 8 - step
        return jnp.concatenate(
            [jnp.where(inside, low_r, high_r), jnp.where(inside, high_r, 0.0)], axis=1
        )
    inside = at >= -step
    return jnp.concatenate(
        [jnp.where(inside, low_r, 0.0), jnp.where(inside, high_r, low_r)], axis=1
    )


def tile_forward(taps, spread, back_hidden, hidden, back_deep):
    def rows(at, carry):
        r = at * RB
        window = spread[pl.ds(r, RB + 4)]
        total = None
        for j in range(TAPS):
            part = None
            for i in range(TAPS):
                term = window[i : i + RB] * taps[i * TAPS + j]
                part = term if part is None else part + term
            part = shifted(part, j - 2)
            total = part if total is None else total + part
        sig = sigmoid(total)
        swish = total * sig
        hidden[pl.ds(r, RB)] = swish.astype(BF16)
        slope = sig + swish * (1.0 - sig)
        back_deep[pl.ds(r + 2, RB)] = back_hidden[pl.ds(r, RB)] * slope
        return carry

    lax.fori_loop(0, H // RB, rows, 0)


def tile_backward(taps, spread, back_deep, pre, back_pre, grad_taps):
    grad_taps[...] = jnp.zeros_like(grad_taps)

    def rows(at, carry):
        r = at * RB
        window = back_deep[pl.ds(r, RB + 4)]
        mine = spread[pl.ds(r + 2, RB)]
        total = None
        for j in range(TAPS):
            moved = shifted(mine, j - 2)
            part = None
            for i in range(TAPS):
                rows_i = window[TAPS - 1 - i : TAPS - 1 - i + RB]
                term = rows_i * taps[i * TAPS + j]
                part = term if part is None else part + term
                prod = rows_i * moved
                prod = prod[:, :8] + prod[:, 8:]
                prod = (prod[0] + prod[1]) + (prod[2] + prod[3])
                grad_taps[i * TAPS + j] += prod
            part = shifted(part, 2 - j)
            total = part if total is None else total + part
        value = pre[pl.ds(r, RB)]
        sig = sigmoid(value)
        slope = sig + value * sig * (1.0 - sig)
        back_pre[pl.ds(r, RB)] = (total * slope).astype(BF16)
        return carry

    lax.fori_loop(0, H // RB, rows, 0)


def exchange(source, landed, send, recv, device):
    copy = pltpu.make_async_remote_copy(
        src_ref=source,
        dst_ref=landed,
        send_sem=send,
        recv_sem=recv,
        device_id=device,
        device_id_type=MESH,
    )
    copy.start()
    return copy


def arrived(source, landed, send, recv, device):
    pltpu.make_async_remote_copy(
        src_ref=source,
        dst_ref=landed,
        send_sem=send,
        recv_sem=recv,
        device_id=device,
        device_id_type=MESH,
    ).wait_recv()


def five_kernel(
    scale, s_ref, cot_ref, exp_ref, dw_ref, proj_ref, out_ref, cots_ref,
    s_pad, cot_pad, pre, spread, bhid, hid, bdeep, bpre, gtaps, gsq, total, back,
    mine, give, got_core, sums, got_space, send_y, got_y, own_z, got_z, pick,
    core_s, core_r, space_s, space_r, y_s, y_r, z_s, z_r, all_s, all_r, cot_s, cot_r, local_sem,
):
    dp, sp = lax.axis_index("dp"), lax.axis_index("space")
    core = lax.rem(dp, CORES)
    z = lax.rem(lax.div(dp, CORES), Z)
    y = lax.div(dp, CORES * Z)
    other = 1 - core
    half = LANES // CORES
    tiles = exp_ref.shape[1] // LANES

    def at_space(place):
        return (dp, place)

    def at_z(place):
        return (dp + (place - z) * CORES, sp)

    def at_y(place):
        return (dp + (place - y) * (CORES * Z), sp)

    sibling = (dp + other - core, sp)
    spaces = [lax.rem(sp + step, GROUP) for step in range(1, GROUP)]
    ys = [lax.rem(y + step, Y) for step in range(1, Y)]
    zs = [lax.rem(z + step, Z) for step in range(1, Z)]

    barrier = pltpu.get_barrier_semaphore()
    everyone = [at_space(p) for p in spaces] + [sibling] + [at_y(p) for p in ys] + [at_z(p) for p in zs]
    for device in everyone:
        pl.semaphore_signal(barrier, inc=1, device_id=device, device_id_type=MESH)

    s_pad[...] = jnp.zeros_like(s_pad)
    cot_pad[...] = jnp.zeros_like(cot_pad)
    s_pad[:, : s_ref.shape[1]] = s_ref[...]
    cot_pad[:, : cot_ref.shape[1]] = cot_ref[...]
    spread[...] = jnp.zeros_like(spread)
    bdeep[...] = jnp.zeros_like(bdeep)
    gsq[...] = jnp.zeros_like(gsq)
    total[...] = jnp.zeros_like(total)
    sums[GROUP - 1, GROUP - 1] = jnp.zeros((half, LANES), BF16)
    pl.semaphore_wait(barrier, len(everyone))

    def put(t, q, block):
        low, high = block[:half], block[half:]
        mine[t, q] = jnp.where(core == 0, low, high)
        give[t, q] = jnp.where(core == 0, high, low).astype(BF16)

    def send_block(owner, slot):
        @pl.when(owner != sp)
        def _():
            exchange(
                sums.at[owner, slot], got_space.at[sp, slot], space_s.at[owner, slot],
                space_r.at[sp, slot], at_space(owner),
            )

    def finish(t):
        arrived(give.at[t], got_core.at[t], core_s.at[t], core_r.at[t], sibling)
        for q in range(SEGS):
            b = t * SEGS + q
            owner, slot = lax.rem(b, GROUP), lax.div(b, GROUP)
            sums[owner, slot] = (mine[t, q] + got_core[t, q].astype(F32)).astype(BF16)
            send_block(owner, slot)

    def tile(t, carry):
        lanes = pl.ds(pl.multiple_of(t * LANES, LANES), LANES)
        exp = exp_ref[:, lanes]
        pre_v = jnp.dot(s_pad[...], exp, preferred_element_type=F32)
        pre[...] = pre_v.reshape(H, W, LANES)
        spread[2 : 2 + H] = (
            (pre_v * sigmoid(pre_v)).astype(BF16).astype(F32).reshape(H, W, LANES)
        )
        bh = lax.dot_general(
            cot_pad[...], proj_ref[lanes], (((1,), (1,)), ((), ())), preferred_element_type=F32
        )
        bhid[...] = bh.reshape(H, W, LANES)
        taps = [dw_ref[k : k + 1, lanes].reshape(1, 1, LANES) for k in range(TAPS * TAPS)]
        tile_forward(taps, spread, bhid, hid, bdeep)
        gp = lax.dot_general(
            hid[...].reshape(H * W, LANES), cot_pad[...], (((0,), (0,)), ((), ())),
            preferred_element_type=F32,
        )
        for q in range(4):
            put(t, q, gp[:, q * LANES : (q + 1) * LANES])
        tile_backward(taps, spread, bdeep, pre, bpre, gtaps)
        bp = bpre[...].reshape(H * W, LANES)
        ge = lax.dot_general(
            bp, s_pad[...], (((0,), (0,)), ((), ())), preferred_element_type=F32
        )
        gsq[DW_AT : DW_AT + TAPS * TAPS] = jnp.sum(gtaps[...], axis=1)
        put(t, 4, ge[:, :LANES])
        put(t, 5, ge[:, LANES : 2 * LANES])
        put(t, 6, ge[:, 2 * LANES :] + gsq[...].T)
        exchange(give.at[t], got_core.at[t], core_s.at[t], core_r.at[t], sibling)
        total[...] += lax.dot_general(
            bp, exp, (((1,), (1,)), ((), ())), preferred_element_type=F32
        )

        @pl.when(t > 0)
        def _():
            finish(t - 1)

        return carry

    lax.fori_loop(0, tiles, tile, 0)
    back[...] = total[...].astype(BF16)
    finish(tiles - 1)
    send_block(GROUP - 1, GROUP - 1)

    rows = back.shape[0] // GROUP

    def rows_of(place):
        return back.at[pl.ds(pl.multiple_of(place * rows, rows), rows)]

    sent = [
        exchange(rows_of(p), cots_ref.at[sp], cot_s.at[p], cot_r.at[sp], at_space(p))
        for p in spaces
    ]
    own = pltpu.make_async_copy(rows_of(sp), cots_ref.at[sp], local_sem)
    own.start()

    for b in range(GROUP // 2):
        pair = []
        for slot in (2 * b, 2 * b + 1):
            for p in spaces:
                arrived(
                    sums.at[p, slot], got_space.at[p, slot], space_s.at[p, slot],
                    space_r.at[p, slot], at_space(p),
                )
            block = sums[sp, slot].astype(F32)
            for p in spaces:
                block += got_space[p, slot].astype(F32)
            pair.append(block.reshape(Y, 8, LANES))
        send_y[:, b] = jnp.concatenate(pair, axis=1).astype(BF16)

    sent += [exchange(send_y.at[p], got_y.at[y], y_s.at[p], y_r.at[y], at_y(p)) for p in ys]
    for p in ys:
        arrived(send_y.at[p], got_y.at[p], y_s.at[p], y_r.at[p], at_y(p))
    summed = send_y[y].astype(F32)
    for p in ys:
        summed += got_y[p].astype(F32)
    own_z[...] = summed

    sent += [exchange(own_z, got_z.at[z], z_s.at[p], z_r.at[z], at_z(p)) for p in zs]
    for p in zs:
        arrived(own_z, got_z.at[p], z_s.at[p], z_r.at[p], at_z(p))
    for p in zs:
        summed += got_z[p]
    summed = (summed * scale).reshape(GROUP, 8, LANES)
    kept = summed[:, :KEEP]
    for p in range(1, Z):
        kept = jnp.where(z == p, summed[:, KEEP * p : KEEP * (p + 1)], kept)
    for b in range(GROUP):
        pick[KEEP * b : KEEP * (b + 1)] = kept[b]

    out_ref[sp] = pick[...]
    sent += [exchange(pick, out_ref.at[sp], all_s.at[p], all_r.at[sp], at_space(p)) for p in spaces]
    for p in spaces:
        arrived(pick, out_ref.at[p], all_s.at[p], all_r.at[p], at_space(p))
    for p in spaces:
        arrived(rows_of(p), cots_ref.at[p], cot_s.at[p], cot_r.at[p], at_space(p))
    own.wait()
    for copy in sent:
        copy.wait_send()

    def drain_core(t, carry):
        pltpu.make_async_remote_copy(
            src_ref=give.at[t], dst_ref=got_core.at[t], send_sem=core_s.at[t],
            recv_sem=core_r.at[t], device_id=sibling, device_id_type=MESH,
        ).wait_send()
        return carry

    lax.fori_loop(0, tiles, drain_core, 0)

    def drain_space(slot, carry):
        for p in spaces:
            pltpu.make_async_remote_copy(
                src_ref=sums.at[p, slot], dst_ref=got_space.at[sp, slot],
                send_sem=space_s.at[p, slot], recv_sem=space_r.at[sp, slot],
                device_id=at_space(p), device_id_type=MESH,
            ).wait_send()
        return carry

    lax.fori_loop(0, GROUP, drain_space, 0)


def five(section_out, cot, expand, taps, project, scale):
    pixels, wide4, wide5 = H * W, 3 * LANES, 4 * LANES
    tiles, half = expand.shape[1] // LANES, LANES // CORES
    vm = pl.BlockSpec(memory_space=pltpu.VMEM)
    dma = pltpu.SemaphoreType.DMA
    return pl.pallas_call(
        functools.partial(five_kernel, scale),
        out_shape=(
            jax.ShapeDtypeStruct((GROUP, GROUP * KEEP, LANES), F32),
            jax.ShapeDtypeStruct((GROUP, pixels // GROUP, wide4), BF16),
        ),
        in_specs=[vm] * 5,
        out_specs=(vm, vm),
        scratch_shapes=[
            pltpu.VMEM((pixels, wide4), BF16),
            pltpu.VMEM((pixels, wide5), BF16),
            pltpu.VMEM((H, W, LANES), F32),
            pltpu.VMEM((H + 4, W, LANES), F32),
            pltpu.VMEM((H, W, LANES), F32),
            pltpu.VMEM((H, W, LANES), BF16),
            pltpu.VMEM((H + 4, W, LANES), F32),
            pltpu.VMEM((H, W, LANES), BF16),
            pltpu.VMEM((TAPS * TAPS, 8, LANES), F32),
            pltpu.VMEM((LANES, LANES), F32),
            pltpu.VMEM((pixels, wide4), F32),
            pltpu.VMEM((pixels, wide4), BF16),
            pltpu.VMEM((tiles, SEGS, half, LANES), F32),
            pltpu.VMEM((tiles, SEGS, half, LANES), BF16),
            pltpu.VMEM((tiles, SEGS, half, LANES), BF16),
            pltpu.VMEM((GROUP, GROUP, half, LANES), BF16),
            pltpu.VMEM((GROUP, GROUP, half, LANES), BF16),
            pltpu.VMEM((Y, GROUP // 2, 16, LANES), BF16),
            pltpu.VMEM((Y, GROUP // 2, 16, LANES), BF16),
            pltpu.VMEM((GROUP // 2, 16, LANES), F32),
            pltpu.VMEM((Z, GROUP // 2, 16, LANES), F32),
            pltpu.VMEM((GROUP * KEEP, LANES), F32),
            dma((tiles,)),
            dma((tiles,)),
            dma((GROUP, GROUP)),
            dma((GROUP, GROUP)),
            dma((Y,)),
            dma((Y,)),
            dma((Z,)),
            dma((Z,)),
            dma((GROUP,)),
            dma((GROUP,)),
            dma((GROUP,)),
            dma((GROUP,)),
            dma(()),
        ],
        compiler_params=pltpu.CompilerParams(
            collective_id=0, has_side_effects=True, vmem_limit_bytes=48 * 1024 * 1024
        ),
        cost_estimate=pl.CostEstimate(
            flops=3_000_000_000, bytes_accessed=8_000_000, transcendentals=1_800_000
        ),
    )(section_out, cot, expand, taps, project)


def channel_order(channels):
    shards = Y * Z * CORES
    each = channels // shards
    order = np.arange(channels).reshape(Y, Z, CORES, each // KEEP, KEEP)
    return order.transpose(3, 2, 0, 1, 4).reshape(-1)


def local(
    expanded,
    dw_four,
    squeeze_down,
    squeeze_up,
    project_four,
    expand_five,
    dw_five,
    project_five,
    cotangent,
):
    group_size = lax.axis_size("space")
    full_rows = expanded.shape[1] * group_size
    cell_count = full_rows * expanded.shape[2]
    c4, channels = expand_five.shape
    c5 = cotangent.shape[3]
    place = (
        lax.broadcasted_iota(jnp.int32, (channels, channels), 0)
        == jnp.asarray(channel_order(channels), jnp.int32)[None, :]
    )
    expand = jnp.dot(
        jnp.pad(expand_five, ((0, 3 * LANES - c4), (0, 0))), place.astype(BF16)
    )
    project = lax.dot_general(
        place.astype(BF16), jnp.pad(project_five, ((0, 0), (0, 4 * LANES - c5))), (((0,), (0,)), ((), ()))
    )
    taps = jnp.dot(dw_five, place.astype(F32), precision="highest")

    padded = padded_2(expanded, "space", 1, 1)
    mixed = swish_act(depthwise(padded, dw_four, 3))
    sums = jnp.sum(mixed, axis=(1, 2))
    row_out = finish_four(mixed, sums, cell_count, squeeze_down, squeeze_up, project_four)
    section_out = lax.all_to_all(row_out, "space", split_axis=0, concat_axis=1, tiled=True)
    total_pixels = (
        cotangent.shape[0] * group_size * lax.axis_size("dp") * full_rows * expanded.shape[2]
    )
    factor = 1.0 / math.sqrt(total_pixels)
    total, cots = five(
        section_out.reshape(H * W, c4), cotangent.reshape(H * W, c5), expand, taps, project, factor
    )
    input_cotangent = cots[:, :, :c4].reshape(group_size, expanded.shape[1], W, c4)
    tiles = channels // LANES
    total = total.reshape(GROUP, GROUP, KEEP, LANES).transpose(1, 0, 2, 3)
    total = total.reshape(GROUP * GROUP, KEEP, LANES)[: tiles * SEGS]
    total = total.reshape(tiles, SEGS, KEEP, LANES).transpose(0, 2, 1, 3)
    total = total.reshape(tiles * KEEP, SEGS * LANES)
    grad_p = total[:, :c5]
    grad_e = total[:, 4 * LANES : 4 * LANES + c4].T
    grad_d = total[:, 6 * LANES + DW_AT : 6 * LANES + DW_AT + TAPS * TAPS].T
    return (grad_e, grad_d, grad_p, input_cotangent)


def solution(mesh):
    in_specs = (
        P("dp", "space", None, None),
        P(),
        P(),
        P(),
        P(),
        P(),
        P(),
        P(),
        P(("dp", "space"), None, None, None),
    )
    out_specs = (P(None, "dp"), P(None, "dp"), P("dp", None), P("dp", "space", None, None))
    return jax.shard_map(local, mesh=mesh, in_specs=in_specs, out_specs=out_specs, check_vma=False)
```

```python
import functools
import math

import jax
import jax.numpy as jnp
from jax import lax
from jax.experimental import pallas as pl
from jax.experimental.pallas import tpu as pltpu
from jax.sharding import PartitionSpec as P

H, W, LANES, RB = 32, 16, 128, 4
TAPS = 5
Y, Z, CORES, KEEP = 8, 4, 2, 2
GROUP = 8
CHUNKS = 4
SEGS = 7
DW_AT = 88
F32, BF16 = jnp.float32, jnp.bfloat16
MESH = pl.DeviceIdType.MESH
ACROSS = (((1,), (1,)), ((), ()))


def sigmoid(value):
    return 0.5 * jnp.tanh(0.5 * value) + 0.5


def shifted(block, step):
    if step == 0:
        return block
    low, high = block[:, :8], block[:, 8:]
    at = lax.broadcasted_iota(jnp.int32, low.shape, 1)
    low_r = pltpu.roll(low, (-step) % 8, 1)
    high_r = pltpu.roll(high, (-step) % 8, 1)
    if step > 0:
        inside = at < 8 - step
        return jnp.concatenate(
            [jnp.where(inside, low_r, high_r), jnp.where(inside, high_r, 0.0)], axis=1
        )
    inside = at >= -step
    return jnp.concatenate(
        [jnp.where(inside, low_r, 0.0), jnp.where(inside, high_r, low_r)], axis=1
    )


def tile_forward(taps, spread, back_hidden, hidden, back_deep):
    def rows(at, carry):
        r = at * RB
        window = spread[pl.ds(r, RB + 4)]
        total = None
        for j in range(TAPS):
            part = None
            for i in range(TAPS):
                term = window[i : i + RB] * taps[i * TAPS + j]
                part = term if part is None else part + term
            part = shifted(part, j - 2)
            total = part if total is None else total + part
        sig = sigmoid(total)
        swish = total * sig
        hidden[pl.ds(r, RB)] = swish.astype(BF16)
        slope = sig + swish * (1.0 - sig)
        back_deep[pl.ds(r + 2, RB)] = back_hidden[pl.ds(r, RB)] * slope
        return carry

    lax.fori_loop(0, H // RB, rows, 0, unroll=True)


def tile_backward(taps, spread, back_deep, pre, back_pre, grad_taps):
    grad_taps[...] = jnp.zeros_like(grad_taps)

    def rows(at, carry):
        r = at * RB
        window = back_deep[pl.ds(r, RB + 4)]
        mine = spread[pl.ds(r + 2, RB)]
        total = None
        for j in range(TAPS):
            moved = shifted(mine, j - 2)
            part = None
            for i in range(TAPS):
                rows_i = window[TAPS - 1 - i : TAPS - 1 - i + RB]
                term = rows_i * taps[i * TAPS + j]
                part = term if part is None else part + term
                prod = rows_i * moved
                prod = prod[:, :8] + prod[:, 8:]
                prod = (prod[0] + prod[1]) + (prod[2] + prod[3])
                grad_taps[i * TAPS + j] += prod
            part = shifted(part, 2 - j)
            total = part if total is None else total + part
        value = pre[pl.ds(r, RB)]
        sig = sigmoid(value)
        slope = sig + value * sig * (1.0 - sig)
        back_pre[pl.ds(r * W, RB * W)] = (total * slope).astype(BF16).reshape(RB * W, LANES)
        return carry

    lax.fori_loop(0, H // RB, rows, 0, unroll=True)


def exchange(source, landed, send, recv, device):
    copy = pltpu.make_async_remote_copy(
        src_ref=source,
        dst_ref=landed,
        send_sem=send,
        recv_sem=recv,
        device_id=device,
        device_id_type=MESH,
    )
    copy.start()
    return copy


def arrived(source, landed, send, recv, device):
    pltpu.make_async_remote_copy(
        src_ref=source,
        dst_ref=landed,
        send_sem=send,
        recv_sem=recv,
        device_id=device,
        device_id_type=MESH,
    ).wait_recv()


def four_rows(x, taps, first, count):
    total = None
    for j in range(3):
        part = None
        for i in range(3):
            term = x[first + i : first + i + count] * taps[3 * i + j]
            part = term if part is None else part + term
        part = shifted(part, j - 1)
        total = part if total is None else total + part
    return total


def one_row(x, taps, i):
    total = None
    for j in range(3):
        part = shifted(x * taps[3 * i + j], j - 1)
        total = part if total is None else total + part
    return total


def kernel(
    scale, x_ref, dw4_ref, down_ref, up_ref, p4_ref, e5_ref, dw5_ref, p5_ref, cot_ref, out_ref, cots_ref,
    low, high, mixed, acc, gates, hid4, rows4, down, up, part, got_part, dw_split, exp_ref, dw_ref, offset, places, proj_ref,
    s_pad, cot_pad, pre, spread, bhid, hid, bdeep, bpre, gtaps, gsq, back,
    mine, give, got_core, sums, got_space, send_y, got_y, own_z, got_z, pick,
    halo_s, halo_r, part_s, part_r, sec_s, sec_r,
    core_s, core_r, space_s, space_r, y_s, y_r, z_s, z_r, all_s, all_r, cot_s, cot_r, local_sem,
):
    dp, sp = lax.axis_index("dp"), lax.axis_index("space")
    core = lax.rem(dp, CORES)
    z = lax.rem(lax.div(dp, CORES), Z)
    y = lax.div(dp, CORES * Z)
    other = 1 - core
    half = LANES // CORES

    def at_space(place):
        return (dp, place)

    def at_z(place):
        return (dp + (place - z) * CORES, sp)

    def at_y(place):
        return (dp + (place - y) * (CORES * Z), sp)

    sibling = (dp + other - core, sp)
    spaces = [lax.rem(sp + step, GROUP) for step in range(1, GROUP)]
    ys = [lax.rem(y + step, Y) for step in range(1, Y)]
    zs = [lax.rem(z + step, Z) for step in range(1, Z)]

    barrier = pltpu.get_barrier_semaphore()
    everyone = [at_space(p) for p in spaces] + [sibling] + [at_y(p) for p in ys] + [at_z(p) for p in zs]
    for device in everyone:
        pl.semaphore_signal(barrier, inc=1, device_id=device, device_id_type=MESH)

    images, local_rows = x_ref.shape[:2]
    channels = x_ref.shape[3]
    chunk = images // CHUNKS
    cells = local_rows * W

    @pl.when(sp == 0)
    def _():
        low[...] = jnp.zeros_like(low)

    @pl.when(sp == GROUP - 1)
    def _():
        high[...] = jnp.zeros_like(high)

    pl.semaphore_wait(barrier, len(everyone))

    def down_copy(c):
        part = pl.ds(c * chunk, chunk)
        return pltpu.make_async_remote_copy(
            src_ref=x_ref.at[part, local_rows - 1], dst_ref=low.at[part], send_sem=halo_s.at[0, c],
            recv_sem=halo_r.at[0, c], device_id=(dp, lax.rem(sp + 1, GROUP)), device_id_type=MESH,
        )

    def up_copy(c):
        part = pl.ds(c * chunk, chunk)
        return pltpu.make_async_remote_copy(
            src_ref=x_ref.at[part, 0], dst_ref=high.at[part], send_sem=halo_s.at[1, c],
            recv_sem=halo_r.at[1, c], device_id=(dp, lax.rem(sp + GROUP - 1, GROUP)), device_id_type=MESH,
        )

    @pl.when(sp < GROUP - 1)
    def _():
        for c in range(CHUNKS):
            down_copy(c).start()

    @pl.when(sp > 0)
    def _():
        for c in range(CHUNKS):
            up_copy(c).start()

    def taps4(t):
        at = slice(t * LANES, (t + 1) * LANES)
        return [dw4_ref[k : k + 1, at].reshape(1, 1, LANES) for k in range(9)]

    def swish_rows(value):
        return value * sigmoid(value)

    def folded(rows):
        rows = rows[:, :8] + rows[:, 8:]
        return rows[0] + rows[1]

    def inner(n, carry):
        for t in range(channels // LANES):
            at = slice(t * LANES, (t + 1) * LANES)
            taps = taps4(t)
            x = x_ref[n, :, :, at].astype(F32)
            none = jnp.zeros((1, W, LANES), F32)
            value = four_rows(jnp.concatenate([none, x, none], axis=0), taps, 0, local_rows)
            done = swish_rows(value[1:3])
            mixed[n, 0:1, :, at] = value[0:1]
            mixed[n, 1:3, :, at] = done
            mixed[n, 3:4, :, at] = value[3:4]
            acc[n, :, at] = folded(done)
        return carry

    lax.fori_loop(0, images, inner, 0)

    down[...] = jnp.zeros_like(down)
    down[: down_ref.shape[0]] = down_ref[...]
    up[...] = jnp.zeros_like(up)
    up[: up_ref.shape[0]] = up_ref[...]
    rows4[...] = jnp.zeros_like(rows4)
    cot_pad[...] = jnp.zeros_like(cot_pad)
    cot_pad[:, : cot_ref.shape[1]] = cot_ref[...]
    exp_ref[...] = jnp.zeros_like(exp_ref)
    proj_ref[...] = jnp.zeros_like(proj_ref)
    spread[...] = jnp.zeros_like(spread)
    bdeep[...] = jnp.zeros_like(bdeep)
    gsq[...] = jnp.zeros_like(gsq)
    sums[GROUP - 1, GROUP - 1] = jnp.zeros((half, LANES), BF16)
    dw_split[...] = jnp.zeros_like(dw_split)
    rest = dw5_ref[...]
    for k in range(3):
        top = rest.astype(BF16)
        dw_split[32 * k : 32 * k + TAPS * TAPS] = top
        rest = rest - top.astype(F32)
    tiles = channels // LANES
    each = channels // (Y * Z * CORES)

    at = lax.broadcasted_iota(jnp.int32, (LANES, channels), 0)
    shard = ((at >> 3) & 7) * (Z * CORES) + ((at >> 1) & 3) * CORES + (at >> 6)
    offset[...] = lax.broadcasted_iota(jnp.int32, (LANES, channels), 1) - shard * each - (at & 1)

    def reorder_expand(t, carry):
        lanes = pl.ds(pl.multiple_of(t * LANES, LANES), LANES)
        place = jnp.where(offset[...] == t * KEEP, 1.0, 0.0).astype(BF16)
        places[lanes] = place
        exp = lax.dot_general(e5_ref[...], place, ACROSS, preferred_element_type=F32)
        exp_ref[: e5_ref.shape[0], lanes] = exp.astype(BF16)
        taps = lax.dot_general(dw_split[...], place, ACROSS, preferred_element_type=F32)
        dw_ref[:, lanes] = taps[:32] + taps[32:64] + taps[64:]
        return carry

    lax.fori_loop(0, tiles, reorder_expand, 0)

    for c in range(CHUNKS):

        @pl.when(sp > 0)
        def _():
            down_copy(c).wait_recv()

        @pl.when(sp < GROUP - 1)
        def _():
            up_copy(c).wait_recv()

        def outer(n, carry):
            for t in range(tiles):
                at = slice(t * LANES, (t + 1) * LANES)
                taps = taps4(t)
                above = low[n, :, at].astype(F32).reshape(1, W, LANES)
                below = high[n, :, at].astype(F32).reshape(1, W, LANES)
                first = swish_rows(mixed[n, 0:1, :, at] + one_row(above, taps, 0))
                last = swish_rows(mixed[n, 3:4, :, at] + one_row(below, taps, 2))
                mixed[n, 0:1, :, at] = first
                mixed[n, 3:4, :, at] = last
                acc[n, :, at] += folded(jnp.concatenate([first, last], axis=0))
            return carry

        lax.fori_loop(c * chunk, (c + 1) * chunk, outer, 0)

    mean = jnp.sum(acc[...], axis=1) / (GROUP * cells)
    top = mean.astype(BF16)
    rest = (mean - top.astype(F32)).astype(BF16)
    value = lax.dot_general(top, down[...], ACROSS, preferred_element_type=F32)
    value += lax.dot_general(rest, down[...], ACROSS, preferred_element_type=F32)
    part[...] = value
    sent = [exchange(part, got_part.at[sp], part_s.at[p], part_r.at[sp], at_space(p)) for p in spaces]
    for h in range(3):
        at = slice(h * channels // 3, (h + 1) * channels // 3)
        proj = lax.dot_general(places[at], p5_ref[...], ACROSS, preferred_element_type=F32)
        proj_ref[at, : p5_ref.shape[0]] = proj.astype(BF16)
    for p in spaces:
        arrived(part, got_part.at[p], part_s.at[p], part_r.at[p], at_space(p))
    for p in spaces:
        value += got_part[p]
    squeezed = swish_rows(value).astype(BF16)
    gates[...] = sigmoid(jnp.dot(squeezed, up[...], preferred_element_type=F32))

    for n in range(images):
        gated = mixed[n].reshape(cells, channels) * gates[n : n + 1]
        hid4[n * cells : (n + 1) * cells] = gated.astype(BF16)

    def rows4_of(place):
        return rows4.at[pl.ds(pl.multiple_of(place * cells, cells), cells)]

    def landing(place):
        return s_pad.at[pl.ds(pl.multiple_of(place * cells, cells), cells)]

    part_rows = images * cells // 2
    for h in range(2):
        at = slice(h * part_rows, (h + 1) * part_rows)
        value = lax.dot_general(hid4[at], p4_ref[...], ACROSS, preferred_element_type=F32)
        rows4[at, : p4_ref.shape[0]] = value.astype(BF16)
        for n in range(h * images // 2, (h + 1) * images // 2):

            @pl.when(sp != n)
            def _():
                exchange(
                    rows4.at[n * cells : (n + 1) * cells], landing(sp), sec_s.at[n], sec_r.at[sp], at_space(n)
                )

    mine_at = pl.ds(pl.multiple_of(sp * cells, cells), cells)
    s_pad[mine_at] = rows4[mine_at]

    def back_hidden(t, carry):
        lanes = pl.ds(pl.multiple_of(t * LANES, LANES), LANES)
        bh = lax.dot_general(
            cot_pad[...], proj_ref[lanes], ACROSS, preferred_element_type=F32
        )
        bhid[t] = bh.reshape(H, W, LANES)
        return carry

    lax.fori_loop(0, tiles, back_hidden, 0)
    for p in spaces:
        arrived(rows4_of(p), landing(p), sec_s.at[p], sec_r.at[p], at_space(p))

    def put(t, q, block):
        low, high = block[:half], block[half:]
        mine[t, q] = jnp.where(core == 0, low, high)
        give[t, q] = jnp.where(core == 0, high, low).astype(BF16)

    def send_block(owner, slot):
        @pl.when(owner != sp)
        def _():
            exchange(
                sums.at[owner, slot], got_space.at[sp, slot], space_s.at[owner, slot],
                space_r.at[sp, slot], at_space(owner),
            )

    def finish(t):
        arrived(give.at[t], got_core.at[t], core_s.at[t], core_r.at[t], sibling)
        for q in range(SEGS):
            b = t * SEGS + q
            owner, slot = lax.rem(b, GROUP), lax.div(b, GROUP)
            sums[owner, slot] = (mine[t, q] + got_core[t, q].astype(F32)).astype(BF16)
            send_block(owner, slot)

    def tile(t, carry):
        lanes = pl.ds(pl.multiple_of(t * LANES, LANES), LANES)
        exp = exp_ref[:, lanes]
        pre_v = jnp.dot(s_pad[...], exp, preferred_element_type=F32)
        pre[...] = pre_v.reshape(H, W, LANES)
        spread[2 : 2 + H] = (
            (pre_v * sigmoid(pre_v)).astype(BF16).astype(F32).reshape(H, W, LANES)
        )
        taps = [dw_ref[k : k + 1, lanes].reshape(1, 1, LANES) for k in range(TAPS * TAPS)]
        tile_forward(taps, spread, bhid.at[t], hid, bdeep)
        gp = lax.dot_general(
            hid[...].reshape(H * W, LANES), cot_pad[...], (((0,), (0,)), ((), ())),
            preferred_element_type=F32,
        )
        for q in range(4):
            put(t, q, gp[:, q * LANES : (q + 1) * LANES])
        tile_backward(taps, spread, bdeep, pre, bpre.at[:, lanes], gtaps)
        bp = bpre[:, lanes]
        ge = lax.dot_general(
            bp, s_pad[...], (((0,), (0,)), ((), ())), preferred_element_type=F32
        )
        gsq[DW_AT : DW_AT + TAPS * TAPS] = jnp.sum(gtaps[...], axis=1)
        put(t, 4, ge[:, :LANES])
        put(t, 5, ge[:, LANES : 2 * LANES])
        put(t, 6, ge[:, 2 * LANES :] + gsq[...].T)
        exchange(give.at[t], got_core.at[t], core_s.at[t], core_r.at[t], sibling)

        @pl.when(t > 0)
        def _():
            finish(t - 1)

        return carry

    lax.fori_loop(0, tiles, tile, 0)
    back[...] = lax.dot_general(
        bpre[...], exp_ref[...], ACROSS, preferred_element_type=F32
    ).astype(BF16)
    finish(tiles - 1)
    send_block(GROUP - 1, GROUP - 1)

    rows = back.shape[0] // GROUP

    def rows_of(place):
        return back.at[pl.ds(pl.multiple_of(place * rows, rows), rows)]

    sent += [
        exchange(rows_of(p), cots_ref.at[sp], cot_s.at[p], cot_r.at[sp], at_space(p))
        for p in spaces
    ]
    own = pltpu.make_async_copy(rows_of(sp), cots_ref.at[sp], local_sem)
    own.start()

    for b in range(GROUP // 2):
        pair = []
        for slot in (2 * b, 2 * b + 1):
            for p in spaces:
                arrived(
                    sums.at[p, slot], got_space.at[p, slot], space_s.at[p, slot],
                    space_r.at[p, slot], at_space(p),
                )
            block = sums[sp, slot].astype(F32)
            for p in spaces:
                block += got_space[p, slot].astype(F32)
            pair.append(block.reshape(Y, 8, LANES))
        send_y[:, b] = jnp.concatenate(pair, axis=1).astype(BF16)

    sent += [exchange(send_y.at[p], got_y.at[y], y_s.at[p], y_r.at[y], at_y(p)) for p in ys]
    for p in ys:
        arrived(send_y.at[p], got_y.at[p], y_s.at[p], y_r.at[p], at_y(p))
    summed = send_y[y].astype(F32)
    for p in ys:
        summed += got_y[p].astype(F32)
    own_z[...] = summed

    sent += [exchange(own_z, got_z.at[z], z_s.at[p], z_r.at[z], at_z(p)) for p in zs]
    for p in zs:
        arrived(own_z, got_z.at[p], z_s.at[p], z_r.at[p], at_z(p))
    for p in zs:
        summed += got_z[p]
    summed = (summed * scale).reshape(GROUP, 8, LANES)
    kept = summed[:, :KEEP]
    for p in range(1, Z):
        kept = jnp.where(z == p, summed[:, KEEP * p : KEEP * (p + 1)], kept)
    for b in range(GROUP):
        pick[KEEP * b : KEEP * (b + 1)] = kept[b]

    out_ref[sp] = pick[...]
    sent += [exchange(pick, out_ref.at[sp], all_s.at[p], all_r.at[sp], at_space(p)) for p in spaces]
    for p in spaces:
        arrived(pick, out_ref.at[p], all_s.at[p], all_r.at[p], at_space(p))
    for p in spaces:
        arrived(rows_of(p), cots_ref.at[p], cot_s.at[p], cot_r.at[p], at_space(p))
    own.wait()
    for copy in sent:
        copy.wait_send()

    def drain_core(t, carry):
        pltpu.make_async_remote_copy(
            src_ref=give.at[t], dst_ref=got_core.at[t], send_sem=core_s.at[t],
            recv_sem=core_r.at[t], device_id=sibling, device_id_type=MESH,
        ).wait_send()
        return carry

    lax.fori_loop(0, tiles, drain_core, 0)

    def drain_space(slot, carry):
        for p in spaces:
            pltpu.make_async_remote_copy(
                src_ref=sums.at[p, slot], dst_ref=got_space.at[sp, slot],
                send_sem=space_s.at[p, slot], recv_sem=space_r.at[sp, slot],
                device_id=at_space(p), device_id_type=MESH,
            ).wait_send()
        return carry

    lax.fori_loop(0, GROUP, drain_space, 0)
    for p in spaces:
        pltpu.make_async_remote_copy(
            src_ref=rows4_of(p), dst_ref=landing(sp), send_sem=sec_s.at[p], recv_sem=sec_r.at[sp],
            device_id=at_space(p), device_id_type=MESH,
        ).wait_send()

    @pl.when(sp < GROUP - 1)
    def _():
        for c in range(CHUNKS):
            down_copy(c).wait_send()

    @pl.when(sp > 0)
    def _():
        for c in range(CHUNKS):
            up_copy(c).wait_send()


def local(
    expanded,
    dw_four,
    squeeze_down,
    squeeze_up,
    project_four,
    expand_five,
    dw_five,
    project_five,
    cotangent,
):
    images, local_rows, _, channels = expanded.shape
    c4, c5 = expand_five.shape[0], cotangent.shape[3]
    pixels, wide4, wide5 = H * W, 3 * LANES, 4 * LANES
    tiles, half = channels // LANES, LANES // CORES
    total_pixels = images * lax.axis_size("dp") * pixels
    vm = pl.BlockSpec(memory_space=pltpu.VMEM)
    dma = pltpu.SemaphoreType.DMA
    vmem = pltpu.VMEM
    total, cots = pl.pallas_call(
        functools.partial(kernel, 1.0 / math.sqrt(total_pixels)),
        out_shape=(
            jax.ShapeDtypeStruct((GROUP, GROUP * KEEP, LANES), F32),
            jax.ShapeDtypeStruct((GROUP, pixels // GROUP, wide4), BF16),
        ),
        in_specs=[vm] * 9,
        out_specs=(vm, vm),
        scratch_shapes=[
            vmem((images, W, channels), BF16),
            vmem((images, W, channels), BF16),
            vmem(expanded.shape, F32),
            vmem((images, 8, channels), F32),
            vmem((images, channels), F32),
            vmem((pixels, channels), BF16),
            vmem((pixels, wide4), BF16),
            vmem((LANES, channels), BF16),
            vmem((LANES, channels), BF16),
            vmem((images, LANES), F32),
            vmem((GROUP, images, LANES), F32),
            vmem((96, channels), BF16),
            vmem((wide4, channels), BF16),
            vmem((32, channels), F32),
            vmem((LANES, channels), jnp.int32),
            vmem((channels, channels), BF16),
            vmem((channels, wide5), BF16),
            vmem((pixels, wide4), BF16),
            vmem((pixels, wide5), BF16),
            vmem((H, W, LANES), F32),
            vmem((H + 4, W, LANES), F32),
            vmem((tiles, H, W, LANES), F32),
            vmem((H, W, LANES), BF16),
            vmem((H + 4, W, LANES), F32),
            vmem((pixels, channels), BF16),
            vmem((TAPS * TAPS, 8, LANES), F32),
            vmem((LANES, LANES), F32),
            vmem((pixels, wide4), BF16),
            vmem((tiles, SEGS, half, LANES), F32),
            vmem((tiles, SEGS, half, LANES), BF16),
            vmem((tiles, SEGS, half, LANES), BF16),
            vmem((GROUP, GROUP, half, LANES), BF16),
            vmem((GROUP, GROUP, half, LANES), BF16),
            vmem((Y, GROUP // 2, 16, LANES), BF16),
            vmem((Y, GROUP // 2, 16, LANES), BF16),
            vmem((GROUP // 2, 16, LANES), F32),
            vmem((Z, GROUP // 2, 16, LANES), F32),
            vmem((GROUP * KEEP, LANES), F32),
            dma((2, CHUNKS)),
            dma((2, CHUNKS)),
            dma((GROUP,)),
            dma((GROUP,)),
            dma((GROUP,)),
            dma((GROUP,)),
            dma((tiles,)),
            dma((tiles,)),
            dma((GROUP, GROUP)),
            dma((GROUP, GROUP)),
            dma((Y,)),
            dma((Y,)),
            dma((Z,)),
            dma((Z,)),
            dma((GROUP,)),
            dma((GROUP,)),
            dma((GROUP,)),
            dma((GROUP,)),
            dma(()),
        ],
        compiler_params=pltpu.CompilerParams(
            collective_id=0, has_side_effects=True, vmem_limit_bytes=56 * 1024 * 1024
        ),
        cost_estimate=pl.CostEstimate(
            flops=3_000_000_000, bytes_accessed=8_000_000, transcendentals=2_400_000
        ),
    )(
        expanded, dw_four, squeeze_down.T, squeeze_up, project_four.T, expand_five, dw_five, project_five.T,
        cotangent.reshape(pixels, c5),
    )
    input_cotangent = cots[:, :, :c4].reshape(images, local_rows, W, c4)
    total = total.reshape(GROUP, GROUP, KEEP, LANES).transpose(1, 0, 2, 3)
    total = total.reshape(GROUP * GROUP, KEEP, LANES)[: tiles * SEGS]
    total = total.reshape(tiles, SEGS, KEEP, LANES).transpose(0, 2, 1, 3)
    total = total.reshape(tiles * KEEP, SEGS * LANES)
    grad_p = total[:, :c5]
    grad_e = total[:, 4 * LANES : 4 * LANES + c4].T
    grad_d = total[:, 6 * LANES + DW_AT : 6 * LANES + DW_AT + TAPS * TAPS].T
    return (grad_e, grad_d, grad_p, input_cotangent)


def solution(mesh):
    in_specs = (
        P("dp", "space", None, None),
        P(),
        P(),
        P(),
        P(),
        P(),
        P(),
        P(),
        P(("dp", "space"), None, None, None),
    )
    out_specs = (P(None, "dp"), P(None, "dp"), P("dp", None), P("dp", "space", None, None))
    return jax.shard_map(local, mesh=mesh, in_specs=in_specs, out_specs=out_specs, check_vma=False)
```

```python
import functools
import math

import jax
import jax.numpy as jnp
from jax import lax
from jax.experimental import pallas as pl
from jax.experimental.pallas import tpu as pltpu
from jax.sharding import PartitionSpec as P

H, W, LANES, RB = 32, 16, 128, 4
TAPS = 5
Y, Z, CORES, KEEP = 8, 4, 2, 2
GROUP = 8
X = 4
CHUNKS = 4
SEGS = 7
DW_AT = 88
F32, BF16 = jnp.float32, jnp.bfloat16
MESH = pl.DeviceIdType.MESH
ACROSS = (((1,), (1,)), ((), ()))


def sigmoid(value):
    return 0.5 * jnp.tanh(0.5 * value) + 0.5


def shifted(block, step):
    if step == 0:
        return block
    low, high = block[:, :8], block[:, 8:]
    at = lax.broadcasted_iota(jnp.int32, low.shape, 1)
    low_r = pltpu.roll(low, (-step) % 8, 1)
    high_r = pltpu.roll(high, (-step) % 8, 1)
    if step > 0:
        inside = at < 8 - step
        return jnp.concatenate(
            [jnp.where(inside, low_r, high_r), jnp.where(inside, high_r, 0.0)], axis=1
        )
    inside = at >= -step
    return jnp.concatenate(
        [jnp.where(inside, low_r, 0.0), jnp.where(inside, high_r, low_r)], axis=1
    )


def tile_forward(taps, spread, back_hidden, hidden, back_deep):
    def rows(at, carry):
        r = at * RB
        window = spread[pl.ds(r, RB + 4)]
        total = None
        for j in range(TAPS):
            part = None
            for i in range(TAPS):
                term = window[i : i + RB] * taps[i * TAPS + j]
                part = term if part is None else part + term
            part = shifted(part, j - 2)
            total = part if total is None else total + part
        sig = sigmoid(total)
        swish = total * sig
        hidden[pl.ds(r, RB)] = swish.astype(BF16)
        slope = sig + swish * (1.0 - sig)
        back_deep[pl.ds(r + 2, RB)] = back_hidden[pl.ds(r, RB)] * slope
        return carry

    lax.fori_loop(0, H // RB, rows, 0, unroll=True)


def tile_backward(taps, spread, back_deep, pre, back_pre, grad_taps):
    grad_taps[...] = jnp.zeros_like(grad_taps)

    def rows(at, carry):
        r = at * RB
        window = back_deep[pl.ds(r, RB + 4)]
        mine = spread[pl.ds(r + 2, RB)]
        total = None
        for j in range(TAPS):
            moved = shifted(mine, j - 2)
            part = None
            for i in range(TAPS):
                rows_i = window[TAPS - 1 - i : TAPS - 1 - i + RB]
                term = rows_i * taps[i * TAPS + j]
                part = term if part is None else part + term
                prod = rows_i * moved
                prod = prod[:, :8] + prod[:, 8:]
                prod = (prod[0] + prod[1]) + (prod[2] + prod[3])
                grad_taps[i * TAPS + j] += prod
            part = shifted(part, 2 - j)
            total = part if total is None else total + part
        value = pre[pl.ds(r, RB)]
        sig = sigmoid(value)
        slope = sig + value * sig * (1.0 - sig)
        back_pre[pl.ds(r * W, RB * W)] = (total * slope).astype(BF16).reshape(RB * W, LANES)
        return carry

    lax.fori_loop(0, H // RB, rows, 0, unroll=True)


def exchange(source, landed, send, recv, device):
    copy = pltpu.make_async_remote_copy(
        src_ref=source,
        dst_ref=landed,
        send_sem=send,
        recv_sem=recv,
        device_id=device,
        device_id_type=MESH,
    )
    copy.start()
    return copy


def arrived(source, landed, send, recv, device):
    pltpu.make_async_remote_copy(
        src_ref=source,
        dst_ref=landed,
        send_sem=send,
        recv_sem=recv,
        device_id=device,
        device_id_type=MESH,
    ).wait_recv()


def four_rows(x, taps, first, count):
    total = None
    for j in range(3):
        part = None
        for i in range(3):
            term = x[first + i : first + i + count] * taps[3 * i + j]
            part = term if part is None else part + term
        part = shifted(part, j - 1)
        total = part if total is None else total + part
    return total


def one_row(x, taps, i):
    total = None
    for j in range(3):
        part = shifted(x * taps[3 * i + j], j - 1)
        total = part if total is None else total + part
    return total


def kernel(
    scale, x_hbm, dw4_hbm, down_hbm, up_hbm, p4_hbm, e5_hbm, dw5_hbm, p5_hbm, cot_hbm, out_ref, cots_ref,
    x_ref, dw4_ref, down_ref, up_ref, p4_ref, e5_ref, dw5_ref, p5_ref, cot_ref, fetch,
    low, high, mixed, acc, gates, hid4, rows4, down, up, part, got_part, dw_split, exp_ref, dw_ref, offset, places, proj_ref,
    s_pad, cot_pad, pre, spread, bhid, hid, bdeep, bpre, gtaps, gsq, back,
    mine, give, got_core, sums, got_space, send_y, got_y, send_z, got_z, pick, got_x,
    halo_s, halo_r, part_s, part_r, sec_s, sec_r,
    core_s, core_r, space_s, space_r, y_s, y_r, z_s, z_r, all_s, all_r, cot_s, cot_r, local_sem,
):
    dp, sp = lax.axis_index("dp"), lax.axis_index("space")
    core = lax.rem(dp, CORES)
    z = lax.rem(lax.div(dp, CORES), Z)
    y = lax.div(dp, CORES * Z)
    other = 1 - core
    half = LANES // CORES

    def at_space(place):
        return (dp, place)

    def at_line(place):
        return (dp + (place[0] - z) * CORES, place[1] * X + x)

    def at_x(place):
        return (dp, z_lo * X + place)

    def at_y(place):
        return (dp + (place - y) * (CORES * Z), sp)

    sibling = (dp + other - core, sp)
    spaces = [lax.rem(sp + step, GROUP) for step in range(1, GROUP)]
    ys = [lax.rem(y + step, Y) for step in range(1, Y)]
    zs = [lax.rem(z + step, Z) for step in range(1, Z)]
    x, z_lo = lax.rem(sp, X), lax.div(sp, X)
    xs = [lax.rem(x + step, X) for step in range(1, X)]
    line = [(z, 1 - z_lo)] + [(p, e) for p in zs for e in range(GROUP // X)]

    barrier = pltpu.get_barrier_semaphore()
    everyone = [at_space(p) for p in spaces] + [sibling] + [at_y(p) for p in ys] + [at_line(p) for p in line[1:]]
    for device in everyone:
        pl.semaphore_signal(barrier, inc=1, device_id=device, device_id_type=MESH)

    def fetched(k, source, target):
        copy = pltpu.make_async_copy(source, target, fetch.at[k])
        copy.start()
        return copy

    x_in = fetched(0, x_hbm, x_ref)
    dw4_in = fetched(1, dw4_hbm, dw4_ref)
    e5_in = fetched(2, e5_hbm, e5_ref)
    dw5_in = fetched(3, dw5_hbm, dw5_ref)
    p5_in = fetched(4, p5_hbm, p5_ref)
    down_in = fetched(5, down_hbm, down_ref)
    up_in = fetched(6, up_hbm, up_ref)
    p4_in = fetched(7, p4_hbm, p4_ref)
    cot_in = fetched(8, cot_hbm, cot_ref)

    images, local_rows = x_ref.shape[:2]
    channels = x_ref.shape[3]
    chunk = images // CHUNKS
    cells = local_rows * W

    @pl.when(sp == 0)
    def _():
        low[...] = jnp.zeros_like(low)

    @pl.when(sp == GROUP - 1)
    def _():
        high[...] = jnp.zeros_like(high)

    pl.semaphore_wait(barrier, len(everyone))

    def down_copy(c):
        part = pl.ds(c * chunk, chunk)
        return pltpu.make_async_remote_copy(
            src_ref=x_hbm.at[part, local_rows - 1], dst_ref=low.at[part], send_sem=halo_s.at[0, c],
            recv_sem=halo_r.at[0, c], device_id=(dp, lax.rem(sp + 1, GROUP)), device_id_type=MESH,
        )

    def up_copy(c):
        part = pl.ds(c * chunk, chunk)
        return pltpu.make_async_remote_copy(
            src_ref=x_hbm.at[part, 0], dst_ref=high.at[part], send_sem=halo_s.at[1, c],
            recv_sem=halo_r.at[1, c], device_id=(dp, lax.rem(sp + GROUP - 1, GROUP)), device_id_type=MESH,
        )

    @pl.when(sp < GROUP - 1)
    def _():
        for c in range(CHUNKS):
            down_copy(c).start()

    @pl.when(sp > 0)
    def _():
        for c in range(CHUNKS):
            up_copy(c).start()

    x_in.wait()
    dw4_in.wait()

    def taps4(t):
        at = slice(t * LANES, (t + 1) * LANES)
        return [dw4_ref[k : k + 1, at].reshape(1, 1, LANES) for k in range(9)]

    def swish_rows(value):
        return value * sigmoid(value)

    def folded(rows):
        rows = rows[:, :8] + rows[:, 8:]
        return rows[0] + rows[1]

    def inner(n, carry):
        for t in range(channels // LANES):
            at = slice(t * LANES, (t + 1) * LANES)
            taps = taps4(t)
            x = x_ref[n, :, :, at].astype(F32)
            none = jnp.zeros((1, W, LANES), F32)
            value = four_rows(jnp.concatenate([none, x, none], axis=0), taps, 0, local_rows)
            done = swish_rows(value[1:3])
            mixed[n, 0:1, :, at] = value[0:1]
            mixed[n, 1:3, :, at] = done
            mixed[n, 3:4, :, at] = value[3:4]
            acc[n, :, at] = folded(done)
        return carry

    lax.fori_loop(0, images, inner, 0)

    e5_in.wait()
    dw5_in.wait()
    down_in.wait()
    up_in.wait()
    cot_in.wait()
    down[...] = jnp.zeros_like(down)
    down[: down_ref.shape[0]] = down_ref[...]
    up[...] = jnp.zeros_like(up)
    up[: up_ref.shape[0]] = up_ref[...]
    rows4[...] = jnp.zeros_like(rows4)
    cot_pad[...] = jnp.zeros_like(cot_pad)
    cot_pad[:, : cot_ref.shape[1]] = cot_ref[...]
    exp_ref[...] = jnp.zeros_like(exp_ref)
    proj_ref[...] = jnp.zeros_like(proj_ref)
    spread[...] = jnp.zeros_like(spread)
    bdeep[...] = jnp.zeros_like(bdeep)
    gsq[...] = jnp.zeros_like(gsq)
    sums[GROUP - 1, GROUP - 1] = jnp.zeros((half, LANES), BF16)
    dw_split[...] = jnp.zeros_like(dw_split)
    rest = dw5_ref[...]
    for k in range(3):
        top = rest.astype(BF16)
        dw_split[32 * k : 32 * k + TAPS * TAPS] = top
        rest = rest - top.astype(F32)
    tiles = channels // LANES
    each = channels // (Y * Z * CORES)

    at = lax.broadcasted_iota(jnp.int32, (LANES, channels), 0)
    shard = ((at >> 3) & 7) * (Z * CORES) + ((at >> 1) & 3) * CORES + (at >> 6)
    offset[...] = lax.broadcasted_iota(jnp.int32, (LANES, channels), 1) - shard * each - (at & 1)

    def reorder_expand(t, carry):
        lanes = pl.ds(pl.multiple_of(t * LANES, LANES), LANES)
        place = jnp.where(offset[...] == t * KEEP, 1.0, 0.0).astype(BF16)
        places[lanes] = place
        exp = lax.dot_general(e5_ref[...], place, ACROSS, preferred_element_type=F32)
        exp_ref[: e5_ref.shape[0], lanes] = exp.astype(BF16)
        taps = lax.dot_general(dw_split[...], place, ACROSS, preferred_element_type=F32)
        dw_ref[:, lanes] = taps[:32] + taps[32:64] + taps[64:]
        return carry

    lax.fori_loop(0, tiles, reorder_expand, 0)

    for c in range(CHUNKS):

        @pl.when(sp > 0)
        def _():
            down_copy(c).wait_recv()

        @pl.when(sp < GROUP - 1)
        def _():
            up_copy(c).wait_recv()

        def outer(n, carry):
            for t in range(tiles):
                at = slice(t * LANES, (t + 1) * LANES)
                taps = taps4(t)
                above = low[n, :, at].astype(F32).reshape(1, W, LANES)
                below = high[n, :, at].astype(F32).reshape(1, W, LANES)
                first = swish_rows(mixed[n, 0:1, :, at] + one_row(above, taps, 0))
                last = swish_rows(mixed[n, 3:4, :, at] + one_row(below, taps, 2))
                mixed[n, 0:1, :, at] = first
                mixed[n, 3:4, :, at] = last
                acc[n, :, at] += folded(jnp.concatenate([first, last], axis=0))
            return carry

        lax.fori_loop(c * chunk, (c + 1) * chunk, outer, 0)

    mean = jnp.sum(acc[...], axis=1) / (GROUP * cells)
    top = mean.astype(BF16)
    rest = (mean - top.astype(F32)).astype(BF16)
    value = lax.dot_general(top, down[...], ACROSS, preferred_element_type=F32)
    value += lax.dot_general(rest, down[...], ACROSS, preferred_element_type=F32)
    part[...] = value
    sent = [exchange(part, got_part.at[sp], part_s.at[p], part_r.at[sp], at_space(p)) for p in spaces]
    p5_in.wait()
    for h in range(3):
        at = slice(h * channels // 3, (h + 1) * channels // 3)
        proj = lax.dot_general(places[at], p5_ref[...], ACROSS, preferred_element_type=F32)
        proj_ref[at, : p5_ref.shape[0]] = proj.astype(BF16)
    for p in spaces:
        arrived(part, got_part.at[p], part_s.at[p], part_r.at[p], at_space(p))
    for p in spaces:
        value += got_part[p]
    squeezed = swish_rows(value).astype(BF16)
    gates[...] = sigmoid(jnp.dot(squeezed, up[...], preferred_element_type=F32))

    for n in range(images):
        gated = mixed[n].reshape(cells, channels) * gates[n : n + 1]
        hid4[n * cells : (n + 1) * cells] = gated.astype(BF16)

    def rows4_of(place):
        return rows4.at[pl.ds(pl.multiple_of(place * cells, cells), cells)]

    def landing(place):
        return s_pad.at[pl.ds(pl.multiple_of(place * cells, cells), cells)]

    p4_in.wait()
    part_rows = images * cells // 2
    for h in range(2):
        at = slice(h * part_rows, (h + 1) * part_rows)
        value = lax.dot_general(hid4[at], p4_ref[...], ACROSS, preferred_element_type=F32)
        rows4[at, : p4_ref.shape[0]] = value.astype(BF16)
        for n in range(h * images // 2, (h + 1) * images // 2):

            @pl.when(sp != n)
            def _():
                exchange(
                    rows4.at[n * cells : (n + 1) * cells], landing(sp), sec_s.at[n], sec_r.at[sp], at_space(n)
                )

    mine_at = pl.ds(pl.multiple_of(sp * cells, cells), cells)
    s_pad[mine_at] = rows4[mine_at]

    def back_hidden(t, carry):
        lanes = pl.ds(pl.multiple_of(t * LANES, LANES), LANES)
        bh = lax.dot_general(
            cot_pad[...], proj_ref[lanes], ACROSS, preferred_element_type=F32
        )
        bhid[t] = bh.reshape(H, W, LANES)
        return carry

    lax.fori_loop(0, tiles, back_hidden, 0)
    for p in spaces:
        arrived(rows4_of(p), landing(p), sec_s.at[p], sec_r.at[p], at_space(p))

    def put(t, q, block):
        low, high = block[:half], block[half:]
        mine[t, q] = jnp.where(core == 0, low, high)
        give[t, q] = jnp.where(core == 0, high, low).astype(BF16)

    def send_block(owner, slot):
        @pl.when(owner != sp)
        def _():
            exchange(
                sums.at[owner, slot], got_space.at[sp, slot], space_s.at[owner, slot],
                space_r.at[sp, slot], at_space(owner),
            )

    def finish(t):
        arrived(give.at[t], got_core.at[t], core_s.at[t], core_r.at[t], sibling)
        for q in range(SEGS):
            b = t * SEGS + q
            owner, slot = lax.rem(b, GROUP), lax.div(b, GROUP)
            sums[owner, slot] = (mine[t, q] + got_core[t, q].astype(F32)).astype(BF16)
            send_block(owner, slot)

    def tile(t, carry):
        lanes = pl.ds(pl.multiple_of(t * LANES, LANES), LANES)
        exp = exp_ref[:, lanes]
        pre_v = jnp.dot(s_pad[...], exp, preferred_element_type=F32)
        pre[...] = pre_v.reshape(H, W, LANES)
        spread[2 : 2 + H] = (
            (pre_v * sigmoid(pre_v)).astype(BF16).astype(F32).reshape(H, W, LANES)
        )
        taps = [dw_ref[k : k + 1, lanes].reshape(1, 1, LANES) for k in range(TAPS * TAPS)]
        tile_forward(taps, spread, bhid.at[t], hid, bdeep)
        gp = lax.dot_general(
            hid[...].reshape(H * W, LANES), cot_pad[...], (((0,), (0,)), ((), ())),
            preferred_element_type=F32,
        )
        for q in range(4):
            put(t, q, gp[:, q * LANES : (q + 1) * LANES])
        tile_backward(taps, spread, bdeep, pre, bpre.at[:, lanes], gtaps)
        bp = bpre[:, lanes]
        ge = lax.dot_general(
            bp, s_pad[...], (((0,), (0,)), ((), ())), preferred_element_type=F32
        )
        gsq[DW_AT : DW_AT + TAPS * TAPS] = jnp.sum(gtaps[...], axis=1)
        put(t, 4, ge[:, :LANES])
        put(t, 5, ge[:, LANES : 2 * LANES])
        put(t, 6, ge[:, 2 * LANES :] + gsq[...].T)
        exchange(give.at[t], got_core.at[t], core_s.at[t], core_r.at[t], sibling)

        @pl.when(t > 0)
        def _():
            finish(t - 1)

        return carry

    lax.fori_loop(0, tiles, tile, 0)
    parts = ((0, GROUP // 2 - 1), (GROUP // 2 - 1, GROUP // 2))

    def gathered(first, last):
        for b in range(first, last):
            pair = []
            for slot in (2 * b, 2 * b + 1):
                for p in spaces:
                    arrived(
                        sums.at[p, slot], got_space.at[p, slot], space_s.at[p, slot],
                        space_r.at[p, slot], at_space(p),
                    )
                block = sums[sp, slot].astype(F32)
                for p in spaces:
                    block += got_space[p, slot].astype(F32)
                pair.append(block.reshape(Y, 8, LANES))
            send_y[:, b] = jnp.concatenate(pair, axis=1).astype(BF16)
        h = parts.index((first, last))
        for p in ys:
            sent.append(
                exchange(
                    send_y.at[p, first:last], got_y.at[y, first:last], y_s.at[h, p], y_r.at[h, y], at_y(p)
                )
            )

    gathered(*parts[0])
    finish(tiles - 1)
    send_block(GROUP - 1, GROUP - 1)
    back[...] = lax.dot_general(
        bpre[...], exp_ref[...], ACROSS, preferred_element_type=F32
    ).astype(BF16)

    rows = back.shape[0] // GROUP

    def rows_of(place):
        return back.at[pl.ds(pl.multiple_of(place * rows, rows), rows)]

    sent += [
        exchange(rows_of(p), cots_ref.at[sp], cot_s.at[p], cot_r.at[sp], at_space(p))
        for p in spaces
    ]
    own = pltpu.make_async_copy(rows_of(sp), cots_ref.at[sp], local_sem)
    own.start()

    gathered(GROUP // 2 - 1, GROUP // 2)
    summed = []
    for h, (first, last) in enumerate(parts):
        for p in ys:
            arrived(send_y.at[p, first:last], got_y.at[p, first:last], y_s.at[h, p], y_r.at[h, p], at_y(p))
        value = send_y[y, first:last].astype(F32)
        for p in ys:
            value += got_y[p, first:last].astype(F32)
        summed.append(value)
    summed = (jnp.concatenate(summed, axis=0) * scale).reshape(GROUP, 8, LANES)

    for p in range(Z):
        for b in range(GROUP):
            send_z[p, KEEP * b : KEEP * (b + 1)] = summed[b, KEEP * p : KEEP * (p + 1)]
    me = z * 2 + z_lo
    sent += [
        exchange(send_z.at[p], got_z.at[me], z_s.at[p, e], z_r.at[me], at_line((p, e))) for p, e in line
    ]
    got_z[me] = send_z[z]
    for p, e in line:
        arrived(send_z.at[p], got_z.at[p * 2 + e], z_s.at[p, e], z_r.at[p * 2 + e], at_line((p, e)))
    for e in range(GROUP // X):
        value = got_z[e]
        for p in range(1, Z):
            value += got_z[p * 2 + e]
        pick[e] = value

    got_x[x] = pick[...]
    sent += [exchange(pick, got_x.at[x], all_s.at[p], all_r.at[x], at_x(p)) for p in xs]
    for p in xs:
        arrived(pick, got_x.at[p], all_s.at[p], all_r.at[p], at_x(p))
    for b in range(tiles * SEGS):
        t, q = divmod(b, SEGS)
        slot, owner = divmod(b, GROUP)
        out_ref[KEEP * t : KEEP * (t + 1), q * LANES : (q + 1) * LANES] = got_x[
            owner % X, owner // X, KEEP * slot : KEEP * (slot + 1)
        ]
    for p in spaces:
        arrived(rows_of(p), cots_ref.at[p], cot_s.at[p], cot_r.at[p], at_space(p))
    own.wait()
    for copy in sent:
        copy.wait_send()

    def drain_core(t, carry):
        pltpu.make_async_remote_copy(
            src_ref=give.at[t], dst_ref=got_core.at[t], send_sem=core_s.at[t],
            recv_sem=core_r.at[t], device_id=sibling, device_id_type=MESH,
        ).wait_send()
        return carry

    lax.fori_loop(0, tiles, drain_core, 0)

    def drain_space(slot, carry):
        for p in spaces:
            pltpu.make_async_remote_copy(
                src_ref=sums.at[p, slot], dst_ref=got_space.at[sp, slot],
                send_sem=space_s.at[p, slot], recv_sem=space_r.at[sp, slot],
                device_id=at_space(p), device_id_type=MESH,
            ).wait_send()
        return carry

    lax.fori_loop(0, GROUP, drain_space, 0)
    for p in spaces:
        pltpu.make_async_remote_copy(
            src_ref=rows4_of(p), dst_ref=landing(sp), send_sem=sec_s.at[p], recv_sem=sec_r.at[sp],
            device_id=at_space(p), device_id_type=MESH,
        ).wait_send()

    @pl.when(sp < GROUP - 1)
    def _():
        for c in range(CHUNKS):
            down_copy(c).wait_send()

    @pl.when(sp > 0)
    def _():
        for c in range(CHUNKS):
            up_copy(c).wait_send()


def place_outputs(total, cots, grad_e, grad_d, grad_p, input_cotangent):
    grad_p[...] = total[:, : grad_p.shape[1]]
    grad_e[...] = total[:, 4 * LANES : 4 * LANES + grad_e.shape[1]]
    grad_d[...] = total[:, 6 * LANES :][:, DW_AT : DW_AT + TAPS * TAPS]
    input_cotangent[...] = cots[:, :, : input_cotangent.shape[3]].reshape(input_cotangent.shape)


def local(
    expanded,
    dw_four,
    squeeze_down,
    squeeze_up,
    project_four,
    expand_five,
    dw_five,
    project_five,
    cotangent,
):
    images, local_rows, _, channels = expanded.shape
    c4, c5 = expand_five.shape[0], cotangent.shape[3]
    pixels, wide4, wide5 = H * W, 3 * LANES, 4 * LANES
    tiles, half = channels // LANES, LANES // CORES
    total_pixels = images * lax.axis_size("dp") * pixels
    vm = pl.BlockSpec(memory_space=pltpu.VMEM)
    dma = pltpu.SemaphoreType.DMA
    vmem = pltpu.VMEM
    operands = (
        expanded, dw_four, squeeze_down.T, squeeze_up, project_four.T, expand_five, dw_five, project_five.T,
        cotangent.reshape(pixels, c5),
    )
    total, cots = pl.pallas_call(
        functools.partial(kernel, 1.0 / math.sqrt(total_pixels)),
        out_shape=(
            jax.ShapeDtypeStruct((tiles * KEEP, SEGS * LANES), F32),
            jax.ShapeDtypeStruct((GROUP, pixels // GROUP, wide4), BF16),
        ),
        in_specs=[pl.BlockSpec(memory_space=pl.ANY)] * 9,
        out_specs=(vm, vm),
        scratch_shapes=[
            *[vmem(a.shape, a.dtype) for a in operands],
            dma((len(operands),)),
            vmem((images, W, channels), BF16),
            vmem((images, W, channels), BF16),
            vmem(expanded.shape, F32),
            vmem((images, 8, channels), F32),
            vmem((images, channels), F32),
            vmem((pixels, channels), BF16),
            vmem((pixels, wide4), BF16),
            vmem((LANES, channels), BF16),
            vmem((LANES, channels), BF16),
            vmem((images, LANES), F32),
            vmem((GROUP, images, LANES), F32),
            vmem((96, channels), BF16),
            vmem((wide4, channels), BF16),
            vmem((32, channels), F32),
            vmem((LANES, channels), jnp.int32),
            vmem((channels, channels), BF16),
            vmem((channels, wide5), BF16),
            vmem((pixels, wide4), BF16),
            vmem((pixels, wide5), BF16),
            vmem((H, W, LANES), F32),
            vmem((H + 4, W, LANES), F32),
            vmem((tiles, H, W, LANES), F32),
            vmem((H, W, LANES), BF16),
            vmem((H + 4, W, LANES), F32),
            vmem((pixels, channels), BF16),
            vmem((TAPS * TAPS, 8, LANES), F32),
            vmem((LANES, LANES), F32),
            vmem((pixels, wide4), BF16),
            vmem((tiles, SEGS, half, LANES), F32),
            vmem((tiles, SEGS, half, LANES), BF16),
            vmem((tiles, SEGS, half, LANES), BF16),
            vmem((GROUP, GROUP, half, LANES), BF16),
            vmem((GROUP, GROUP, half, LANES), BF16),
            vmem((Y, GROUP // 2, 16, LANES), BF16),
            vmem((Y, GROUP // 2, 16, LANES), BF16),
            vmem((Z, GROUP * KEEP, LANES), F32),
            vmem((2 * Z, GROUP * KEEP, LANES), F32),
            vmem((GROUP // X, GROUP * KEEP, LANES), F32),
            vmem((X, GROUP // X, GROUP * KEEP, LANES), F32),
            dma((2, CHUNKS)),
            dma((2, CHUNKS)),
            dma((GROUP,)),
            dma((GROUP,)),
            dma((GROUP,)),
            dma((GROUP,)),
            dma((tiles,)),
            dma((tiles,)),
            dma((GROUP, GROUP)),
            dma((GROUP, GROUP)),
            dma((2, Y)),
            dma((2, Y)),
            dma((Z, 2)),
            dma((2 * Z,)),
            dma((X,)),
            dma((X,)),
            dma((GROUP,)),
            dma((GROUP,)),
            dma(()),
        ],
        compiler_params=pltpu.CompilerParams(
            collective_id=0, has_side_effects=True, vmem_limit_bytes=56 * 1024 * 1024
        ),
        cost_estimate=pl.CostEstimate(
            flops=3_000_000_000, bytes_accessed=8_000_000, transcendentals=2_400_000
        ),
    )(*operands)
    grad_e, grad_d, grad_p, input_cotangent = pl.pallas_call(
        place_outputs,
        out_shape=(
            jax.ShapeDtypeStruct((tiles * KEEP, c4), F32),
            jax.ShapeDtypeStruct((tiles * KEEP, TAPS * TAPS), F32),
            jax.ShapeDtypeStruct((tiles * KEEP, c5), F32),
            jax.ShapeDtypeStruct((images, local_rows, W, c4), BF16),
        ),
        in_specs=[vm, vm],
        out_specs=(vm, vm, vm, vm),
    )(total, cots)
    return (grad_e.T, grad_d.T, grad_p, input_cotangent)


def solution(mesh):
    in_specs = (
        P("dp", "space", None, None),
        P(),
        P(),
        P(),
        P(),
        P(),
        P(),
        P(),
        P(("dp", "space"), None, None, None),
    )
    out_specs = (P(None, "dp"), P(None, "dp"), P("dp", None), P("dp", "space", None, None))
    return jax.shard_map(local, mesh=mesh, in_specs=in_specs, out_specs=out_specs, check_vma=False)
```

```python
import functools
import math

import jax
import jax.numpy as jnp
from jax import lax
from jax.experimental import pallas as pl
from jax.experimental.pallas import tpu as pltpu
from jax.sharding import PartitionSpec as P

H, W, LANES, RB = 32, 16, 128, 4
TAPS = 5
Y, Z, CORES, KEEP = 8, 4, 2, 2
GROUP = 8
X = 4
ORDER = (2, 6, 4, 1, 7, 3, 5, 0)
CHUNKS = 4
SEGS = 7
DW_AT = 88
F32, BF16 = jnp.float32, jnp.bfloat16
MESH = pl.DeviceIdType.MESH
ACROSS = (((1,), (1,)), ((), ()))


def sigmoid(value):
    return 0.5 * jnp.tanh(0.5 * value) + 0.5


def shifted(block, step):
    if step == 0:
        return block
    low, high = block[:, :8], block[:, 8:]
    at = lax.broadcasted_iota(jnp.int32, low.shape, 1)
    low_r = pltpu.roll(low, (-step) % 8, 1)
    high_r = pltpu.roll(high, (-step) % 8, 1)
    if step > 0:
        inside = at < 8 - step
        return jnp.concatenate(
            [jnp.where(inside, low_r, high_r), jnp.where(inside, high_r, 0.0)], axis=1
        )
    inside = at >= -step
    return jnp.concatenate(
        [jnp.where(inside, low_r, 0.0), jnp.where(inside, high_r, low_r)], axis=1
    )


def tile_forward(taps, spread, back_hidden, hidden, back_deep):
    def rows(at, carry):
        r = at * RB
        window = spread[pl.ds(r, RB + 4)]
        total = None
        for j in range(TAPS):
            part = None
            for i in range(TAPS):
                term = window[i : i + RB] * taps[i * TAPS + j]
                part = term if part is None else part + term
            part = shifted(part, j - 2)
            total = part if total is None else total + part
        sig = sigmoid(total)
        swish = total * sig
        hidden[pl.ds(r, RB)] = swish.astype(BF16)
        slope = sig + swish * (1.0 - sig)
        back_deep[pl.ds(r + 2, RB)] = back_hidden[pl.ds(r, RB)] * slope
        return carry

    lax.fori_loop(0, H // RB, rows, 0, unroll=True)


def tile_backward(taps, spread, back_deep, pre, back_pre, grad_taps):
    grad_taps[...] = jnp.zeros_like(grad_taps)

    def rows(at, carry):
        r = at * RB
        window = back_deep[pl.ds(r, RB + 4)]
        mine = spread[pl.ds(r + 2, RB)]
        total = None
        for j in range(TAPS):
            moved = shifted(mine, j - 2)
            part = None
            for i in range(TAPS):
                rows_i = window[TAPS - 1 - i : TAPS - 1 - i + RB]
                term = rows_i * taps[i * TAPS + j]
                part = term if part is None else part + term
                prod = rows_i * moved
                prod = prod[:, :8] + prod[:, 8:]
                prod = (prod[0] + prod[1]) + (prod[2] + prod[3])
                grad_taps[i * TAPS + j] += prod
            part = shifted(part, 2 - j)
            total = part if total is None else total + part
        value = pre[pl.ds(r, RB)]
        sig = sigmoid(value)
        slope = sig + value * sig * (1.0 - sig)
        back_pre[pl.ds(r * W, RB * W)] = (total * slope).astype(BF16).reshape(RB * W, LANES)
        return carry

    lax.fori_loop(0, H // RB, rows, 0, unroll=True)


def exchange(source, landed, send, recv, device):
    copy = pltpu.make_async_remote_copy(
        src_ref=source,
        dst_ref=landed,
        send_sem=send,
        recv_sem=recv,
        device_id=device,
        device_id_type=MESH,
    )
    copy.start()
    return copy


def arrived(source, landed, send, recv, device):
    pltpu.make_async_remote_copy(
        src_ref=source,
        dst_ref=landed,
        send_sem=send,
        recv_sem=recv,
        device_id=device,
        device_id_type=MESH,
    ).wait_recv()


def four_rows(x, taps, first, count):
    total = None
    for j in range(3):
        part = None
        for i in range(3):
            term = x[first + i : first + i + count] * taps[3 * i + j]
            part = term if part is None else part + term
        part = shifted(part, j - 1)
        total = part if total is None else total + part
    return total


def one_row(x, taps, i):
    total = None
    for j in range(3):
        part = shifted(x * taps[3 * i + j], j - 1)
        total = part if total is None else total + part
    return total


def kernel(
    scale, x_hbm, dw4_hbm, down_hbm, up_hbm, p4_hbm, e5_hbm, dw5_hbm, p5_hbm, cot_hbm, out_ref, cots_ref,
    x_ref, dw4_ref, down_ref, up_ref, p4_ref, e5_ref, dw5_ref, p5_ref, cot_ref, fetch,
    low, high, mixed, acc, gates, hid4, rows4, down, up, part, got_part, dw_split, exp_ref, dw_ref, offset, places, proj_ref,
    s_pad, cot_pad, pre, spread, bhid, hid, bdeep, bpre, gtaps, gsq, back,
    mine, give, got_core, sums, got_space, send_y, got_y, send_z, got_z, pick, got_x,
    halo_s, halo_r, part_s, part_r, sec_s, sec_r,
    core_s, core_r, space_s, space_r, y_s, y_r, z_s, z_r, all_s, all_r, cot_s, cot_r, local_sem,
):
    dp, sp = lax.axis_index("dp"), lax.axis_index("space")
    core = lax.rem(dp, CORES)
    z = lax.rem(lax.div(dp, CORES), Z)
    y = lax.div(dp, CORES * Z)
    other = 1 - core
    half = LANES // CORES

    def at_space(place):
        return (dp, place)

    def at_line(place):
        return (dp + (place[0] - z) * CORES, place[1] * X + x)

    def at_x(place):
        return (dp, z_lo * X + place)

    def at_y(place):
        return (dp + (place - y) * (CORES * Z), sp)

    sibling = (dp + other - core, sp)
    spaces = [lax.rem(sp + step, GROUP) for step in range(1, GROUP)]
    ys = [lax.rem(y + step, Y) for step in range(1, Y)]
    zs = [lax.rem(z + step, Z) for step in range(1, Z)]
    x, z_lo = lax.rem(sp, X), lax.div(sp, X)
    xs = [lax.rem(x + step, X) for step in range(1, X)]
    line = [(z, 1 - z_lo)] + [(p, e) for p in zs for e in range(GROUP // X)]

    barrier = pltpu.get_barrier_semaphore()
    everyone = [at_space(p) for p in spaces] + [sibling] + [at_y(p) for p in ys] + [at_line(p) for p in line[1:]]
    for device in everyone:
        pl.semaphore_signal(barrier, inc=1, device_id=device, device_id_type=MESH)

    def fetched(k, source, target):
        copy = pltpu.make_async_copy(source, target, fetch.at[k])
        copy.start()
        return copy

    x_in = fetched(0, x_hbm, x_ref)
    dw4_in = fetched(1, dw4_hbm, dw4_ref)
    e5_in = fetched(2, e5_hbm, e5_ref)
    dw5_in = fetched(3, dw5_hbm, dw5_ref)
    p5_in = fetched(4, p5_hbm, p5_ref)
    down_in = fetched(5, down_hbm, down_ref)
    up_in = fetched(6, up_hbm, up_ref)
    p4_in = fetched(7, p4_hbm, p4_ref)
    cot_in = fetched(8, cot_hbm, cot_ref)

    images, local_rows = x_ref.shape[:2]
    channels = x_ref.shape[3]
    chunk = images // CHUNKS
    cells = local_rows * W

    @pl.when(sp == 0)
    def _():
        low[...] = jnp.zeros_like(low)

    @pl.when(sp == GROUP - 1)
    def _():
        high[...] = jnp.zeros_like(high)

    pl.semaphore_wait(barrier, len(everyone))

    def down_copy(c):
        part = pl.ds(c * chunk, chunk)
        return pltpu.make_async_remote_copy(
            src_ref=x_hbm.at[part, local_rows - 1], dst_ref=low.at[part], send_sem=halo_s.at[0, c],
            recv_sem=halo_r.at[0, c], device_id=(dp, lax.rem(sp + 1, GROUP)), device_id_type=MESH,
        )

    def up_copy(c):
        part = pl.ds(c * chunk, chunk)
        return pltpu.make_async_remote_copy(
            src_ref=x_hbm.at[part, 0], dst_ref=high.at[part], send_sem=halo_s.at[1, c],
            recv_sem=halo_r.at[1, c], device_id=(dp, lax.rem(sp + GROUP - 1, GROUP)), device_id_type=MESH,
        )

    @pl.when(sp < GROUP - 1)
    def _():
        for c in range(CHUNKS):
            down_copy(c).start()

    @pl.when(sp > 0)
    def _():
        for c in range(CHUNKS):
            up_copy(c).start()

    x_in.wait()
    dw4_in.wait()

    def taps4(t):
        at = slice(t * LANES, (t + 1) * LANES)
        return [dw4_ref[k : k + 1, at].reshape(1, 1, LANES) for k in range(9)]

    def swish_rows(value):
        return value * sigmoid(value)

    def folded(rows):
        rows = rows[:, :8] + rows[:, 8:]
        return rows[0] + rows[1]

    def inner(n, carry):
        for t in range(channels // LANES):
            at = slice(t * LANES, (t + 1) * LANES)
            taps = taps4(t)
            x = x_ref[n, :, :, at].astype(F32)
            none = jnp.zeros((1, W, LANES), F32)
            value = four_rows(jnp.concatenate([none, x, none], axis=0), taps, 0, local_rows)
            done = swish_rows(value[1:3])
            mixed[n, 0:1, :, at] = value[0:1]
            mixed[n, 1:3, :, at] = done
            mixed[n, 3:4, :, at] = value[3:4]
            acc[n, :, at] = folded(done)
        return carry

    lax.fori_loop(0, images, inner, 0)

    e5_in.wait()
    dw5_in.wait()
    down_in.wait()
    up_in.wait()
    cot_in.wait()
    down[...] = jnp.zeros_like(down)
    down[: down_ref.shape[0]] = down_ref[...]
    up[...] = jnp.zeros_like(up)
    up[: up_ref.shape[0]] = up_ref[...]
    rows4[...] = jnp.zeros_like(rows4)
    cot_pad[...] = jnp.zeros_like(cot_pad)
    cot_pad[:, : cot_ref.shape[1]] = cot_ref[...]
    exp_ref[...] = jnp.zeros_like(exp_ref)
    proj_ref[...] = jnp.zeros_like(proj_ref)
    spread[...] = jnp.zeros_like(spread)
    bdeep[...] = jnp.zeros_like(bdeep)
    gsq[...] = jnp.zeros_like(gsq)
    sums[GROUP - 1, GROUP - 1] = jnp.zeros((half, LANES), BF16)
    dw_split[...] = jnp.zeros_like(dw_split)
    rest = dw5_ref[...]
    for k in range(3):
        top = rest.astype(BF16)
        dw_split[32 * k : 32 * k + TAPS * TAPS] = top
        rest = rest - top.astype(F32)
    tiles = channels // LANES
    each = channels // (Y * Z * CORES)

    at = lax.broadcasted_iota(jnp.int32, (LANES, channels), 0)
    shard = ((at >> 3) & 7) * (Z * CORES) + ((at >> 1) & 3) * CORES + (at >> 6)
    offset[...] = lax.broadcasted_iota(jnp.int32, (LANES, channels), 1) - shard * each - (at & 1)

    def reorder_expand(t, carry):
        lanes = pl.ds(pl.multiple_of(t * LANES, LANES), LANES)
        place = jnp.where(offset[...] == t * KEEP, 1.0, 0.0).astype(BF16)
        places[lanes] = place
        exp = lax.dot_general(e5_ref[...], place, ACROSS, preferred_element_type=F32)
        exp_ref[: e5_ref.shape[0], lanes] = exp.astype(BF16)
        taps = lax.dot_general(dw_split[...], place, ACROSS, preferred_element_type=F32)
        dw_ref[:, lanes] = taps[:32] + taps[32:64] + taps[64:]
        return carry

    lax.fori_loop(0, tiles, reorder_expand, 0)

    for c in range(CHUNKS):

        @pl.when(sp > 0)
        def _():
            down_copy(c).wait_recv()

        @pl.when(sp < GROUP - 1)
        def _():
            up_copy(c).wait_recv()

        def outer(n, carry):
            for t in range(tiles):
                at = slice(t * LANES, (t + 1) * LANES)
                taps = taps4(t)
                above = low[n, :, at].astype(F32).reshape(1, W, LANES)
                below = high[n, :, at].astype(F32).reshape(1, W, LANES)
                first = swish_rows(mixed[n, 0:1, :, at] + one_row(above, taps, 0))
                last = swish_rows(mixed[n, 3:4, :, at] + one_row(below, taps, 2))
                mixed[n, 0:1, :, at] = first
                mixed[n, 3:4, :, at] = last
                acc[n, :, at] += folded(jnp.concatenate([first, last], axis=0))
            return carry

        lax.fori_loop(c * chunk, (c + 1) * chunk, outer, 0)

    mean = jnp.sum(acc[...], axis=1) / (GROUP * cells)
    top = mean.astype(BF16)
    rest = (mean - top.astype(F32)).astype(BF16)
    value = lax.dot_general(top, down[...], ACROSS, preferred_element_type=F32)
    value += lax.dot_general(rest, down[...], ACROSS, preferred_element_type=F32)
    part[...] = value
    sent = [exchange(part, got_part.at[sp], part_s.at[p], part_r.at[sp], at_space(p)) for p in spaces]
    p5_in.wait()

    def reorder_project(h):
        at = slice(h * channels // 3, (h + 1) * channels // 3)
        proj = lax.dot_general(places[at], p5_ref[...], ACROSS, preferred_element_type=F32)
        proj_ref[at, : p5_ref.shape[0]] = proj.astype(BF16)

    reorder_project(0)
    reorder_project(1)
    for p in spaces:
        arrived(part, got_part.at[p], part_s.at[p], part_r.at[p], at_space(p))
    for p in spaces:
        value += got_part[p]
    squeezed = swish_rows(value).astype(BF16)
    gates[...] = sigmoid(jnp.dot(squeezed, up[...], preferred_element_type=F32))

    order = [lax.rem(sp + step, GROUP) for step in ORDER]
    for k, n in enumerate(order):
        gated = mixed[n].reshape(cells, channels) * gates[pl.ds(n, 1)]
        hid4[k * cells : (k + 1) * cells] = gated.astype(BF16)

    def rows4_of(k):
        return rows4.at[k * cells : (k + 1) * cells]

    def landing(place):
        return s_pad.at[pl.ds(pl.multiple_of(place * cells, cells), cells)]

    p4_in.wait()
    part_rows = images * cells // 2
    for h in range(2):
        at = slice(h * part_rows, (h + 1) * part_rows)
        value = lax.dot_general(hid4[at], p4_ref[...], ACROSS, preferred_element_type=F32)
        rows4[at, : p4_ref.shape[0]] = value.astype(BF16)
        for k in range(h * images // 2, min((h + 1) * images // 2, images - 1)):
            n = order[k]
            exchange(rows4_of(k), landing(sp), sec_s.at[n], sec_r.at[sp], at_space(n))

    mine_at = pl.ds(pl.multiple_of(sp * cells, cells), cells)
    s_pad[mine_at] = rows4[(images - 1) * cells :]

    reorder_project(2)

    def back_hidden(t, carry):
        lanes = pl.ds(pl.multiple_of(t * LANES, LANES), LANES)
        bh = lax.dot_general(
            cot_pad[...], proj_ref[lanes], ACROSS, preferred_element_type=F32
        )
        bhid[t] = bh.reshape(H, W, LANES)
        return carry

    lax.fori_loop(0, tiles, back_hidden, 0)
    for p in spaces:
        arrived(rows4_of(0), landing(p), sec_s.at[p], sec_r.at[p], at_space(p))

    for h in range(3):
        wide = channels // 3
        value = jnp.dot(s_pad[...], exp_ref[:, h * wide : (h + 1) * wide], preferred_element_type=F32)
        for t in range(tiles // 3):
            pre[h * (tiles // 3) + t] = value[:, t * LANES : (t + 1) * LANES].reshape(H, W, LANES)

    def put(t, q, block):
        low, high = block[:half], block[half:]
        mine[t, q] = jnp.where(core == 0, low, high)
        give[t, q] = jnp.where(core == 0, high, low).astype(BF16)

    def send_block(owner, slot):
        @pl.when(owner != sp)
        def _():
            exchange(
                sums.at[owner, slot], got_space.at[sp, slot], space_s.at[owner, slot],
                space_r.at[sp, slot], at_space(owner),
            )

    def finish(t):
        arrived(give.at[t], got_core.at[t], core_s.at[t], core_r.at[t], sibling)
        for step in range(SEGS):
            q = lax.rem(sp + step, SEGS)
            b = t * SEGS + q
            owner, slot = lax.rem(b, GROUP), lax.div(b, GROUP)
            sums[owner, slot] = (mine[t, q] + got_core[t, q].astype(F32)).astype(BF16)
            send_block(owner, slot)

    def tile(t, carry):
        lanes = pl.ds(pl.multiple_of(t * LANES, LANES), LANES)
        pre_v = pre[t]
        spread[2 : 2 + H] = (pre_v * sigmoid(pre_v)).astype(BF16).astype(F32)
        taps = [dw_ref[k : k + 1, lanes].reshape(1, 1, LANES) for k in range(TAPS * TAPS)]
        tile_forward(taps, spread, bhid.at[t], hid, bdeep)
        gp = lax.dot_general(
            hid[...].reshape(H * W, LANES), cot_pad[...], (((0,), (0,)), ((), ())),
            preferred_element_type=F32,
        )
        for q in range(4):
            put(t, q, gp[:, q * LANES : (q + 1) * LANES])
        tile_backward(taps, spread, bdeep, pre.at[t], bpre.at[:, lanes], gtaps)
        bp = bpre[:, lanes]
        ge = lax.dot_general(
            bp, s_pad[...], (((0,), (0,)), ((), ())), preferred_element_type=F32
        )
        gsq[DW_AT : DW_AT + TAPS * TAPS] = jnp.sum(gtaps[...], axis=1)
        put(t, 4, ge[:, :LANES])
        put(t, 5, ge[:, LANES : 2 * LANES])
        put(t, 6, ge[:, 2 * LANES :] + gsq[...].T)
        exchange(give.at[t], got_core.at[t], core_s.at[t], core_r.at[t], sibling)

        @pl.when(t > 0)
        def _():
            finish(t - 1)

        return carry

    lax.fori_loop(0, tiles, tile, 0)
    parts = ((0, GROUP // 2 - 1), (GROUP // 2 - 1, GROUP // 2))

    def gathered(first, last):
        for b in range(first, last):
            pair = []
            for slot in (2 * b, 2 * b + 1):
                for p in spaces:
                    arrived(
                        sums.at[p, slot], got_space.at[p, slot], space_s.at[p, slot],
                        space_r.at[p, slot], at_space(p),
                    )
                block = sums[sp, slot].astype(F32)
                for p in spaces:
                    block += got_space[p, slot].astype(F32)
                pair.append(block.reshape(Y, 8, LANES))
            send_y[:, b] = jnp.concatenate(pair, axis=1).astype(BF16)
        h = parts.index((first, last))
        for p in ys:
            sent.append(
                exchange(
                    send_y.at[p, first:last], got_y.at[y, first:last], y_s.at[h, p], y_r.at[h, y], at_y(p)
                )
            )

    gathered(*parts[0])
    finish(tiles - 1)
    send_block(GROUP - 1, GROUP - 1)
    back[...] = lax.dot_general(
        bpre[...], exp_ref[...], ACROSS, preferred_element_type=F32
    ).astype(BF16)

    rows = back.shape[0] // GROUP

    def rows_of(place):
        return back.at[pl.ds(pl.multiple_of(place * rows, rows), rows)]

    sent += [
        exchange(rows_of(p), cots_ref.at[sp], cot_s.at[p], cot_r.at[sp], at_space(p))
        for p in spaces
    ]
    own = pltpu.make_async_copy(rows_of(sp), cots_ref.at[sp], local_sem)
    own.start()

    gathered(GROUP // 2 - 1, GROUP // 2)
    summed = []
    for h, (first, last) in enumerate(parts):
        for p in ys:
            arrived(send_y.at[p, first:last], got_y.at[p, first:last], y_s.at[h, p], y_r.at[h, p], at_y(p))
        value = send_y[y, first:last].astype(F32)
        for p in ys:
            value += got_y[p, first:last].astype(F32)
        summed.append(value)
    summed = (jnp.concatenate(summed, axis=0) * scale).reshape(GROUP, 8, LANES)

    for p in range(Z):
        for b in range(GROUP):
            send_z[p, KEEP * b : KEEP * (b + 1)] = summed[b, KEEP * p : KEEP * (p + 1)]
    me = z * 2 + z_lo
    sent += [
        exchange(send_z.at[p], got_z.at[me], z_s.at[p, e], z_r.at[me], at_line((p, e))) for p, e in line
    ]
    got_z[me] = send_z[z]
    for p, e in line:
        arrived(send_z.at[p], got_z.at[p * 2 + e], z_s.at[p, e], z_r.at[p * 2 + e], at_line((p, e)))
    for e in range(GROUP // X):
        value = got_z[e]
        for p in range(1, Z):
            value += got_z[p * 2 + e]
        pick[e] = value

    got_x[x] = pick[...]
    sent += [exchange(pick, got_x.at[x], all_s.at[p], all_r.at[x], at_x(p)) for p in xs]
    for p in xs:
        arrived(pick, got_x.at[p], all_s.at[p], all_r.at[p], at_x(p))
    for b in range(tiles * SEGS):
        t, q = divmod(b, SEGS)
        slot, owner = divmod(b, GROUP)
        out_ref[KEEP * t : KEEP * (t + 1), q * LANES : (q + 1) * LANES] = got_x[
            owner % X, owner // X, KEEP * slot : KEEP * (slot + 1)
        ]
    for p in spaces:
        arrived(rows_of(p), cots_ref.at[p], cot_s.at[p], cot_r.at[p], at_space(p))
    own.wait()
    for copy in sent:
        copy.wait_send()

    def drain_core(t, carry):
        pltpu.make_async_remote_copy(
            src_ref=give.at[t], dst_ref=got_core.at[t], send_sem=core_s.at[t],
            recv_sem=core_r.at[t], device_id=sibling, device_id_type=MESH,
        ).wait_send()
        return carry

    lax.fori_loop(0, tiles, drain_core, 0)

    def drain_space(slot, carry):
        for p in spaces:
            pltpu.make_async_remote_copy(
                src_ref=sums.at[p, slot], dst_ref=got_space.at[sp, slot],
                send_sem=space_s.at[p, slot], recv_sem=space_r.at[sp, slot],
                device_id=at_space(p), device_id_type=MESH,
            ).wait_send()
        return carry

    lax.fori_loop(0, GROUP, drain_space, 0)
    for p in spaces:
        pltpu.make_async_remote_copy(
            src_ref=rows4_of(0), dst_ref=landing(sp), send_sem=sec_s.at[p], recv_sem=sec_r.at[sp],
            device_id=at_space(p), device_id_type=MESH,
        ).wait_send()

    @pl.when(sp < GROUP - 1)
    def _():
        for c in range(CHUNKS):
            down_copy(c).wait_send()

    @pl.when(sp > 0)
    def _():
        for c in range(CHUNKS):
            up_copy(c).wait_send()


def place_outputs(total, cots, grad_e, grad_d, grad_p, input_cotangent):
    grad_p[...] = total[:, : grad_p.shape[1]]
    grad_e[...] = total[:, 4 * LANES : 4 * LANES + grad_e.shape[1]]
    grad_d[...] = total[:, 6 * LANES :][:, DW_AT : DW_AT + TAPS * TAPS]
    input_cotangent[...] = cots[:, :, : input_cotangent.shape[3]].reshape(input_cotangent.shape)


def local(
    expanded,
    dw_four,
    squeeze_down,
    squeeze_up,
    project_four,
    expand_five,
    dw_five,
    project_five,
    cotangent,
):
    images, local_rows, _, channels = expanded.shape
    c4, c5 = expand_five.shape[0], cotangent.shape[3]
    pixels, wide4, wide5 = H * W, 3 * LANES, 4 * LANES
    tiles, half = channels // LANES, LANES // CORES
    total_pixels = images * lax.axis_size("dp") * pixels
    vm = pl.BlockSpec(memory_space=pltpu.VMEM)
    dma = pltpu.SemaphoreType.DMA
    vmem = pltpu.VMEM
    operands = (
        expanded, dw_four, squeeze_down.T, squeeze_up, project_four.T, expand_five, dw_five, project_five.T,
        cotangent.reshape(pixels, c5),
    )
    total, cots = pl.pallas_call(
        functools.partial(kernel, 1.0 / math.sqrt(total_pixels)),
        out_shape=(
            jax.ShapeDtypeStruct((tiles * KEEP, SEGS * LANES), F32),
            jax.ShapeDtypeStruct((GROUP, pixels // GROUP, wide4), BF16),
        ),
        in_specs=[pl.BlockSpec(memory_space=pl.ANY)] * 9,
        out_specs=(vm, vm),
        scratch_shapes=[
            *[vmem(a.shape, a.dtype) for a in operands],
            dma((len(operands),)),
            vmem((images, W, channels), BF16),
            vmem((images, W, channels), BF16),
            vmem(expanded.shape, F32),
            vmem((images, 8, channels), F32),
            vmem((images, channels), F32),
            vmem((pixels, channels), BF16),
            vmem((pixels, wide4), BF16),
            vmem((LANES, channels), BF16),
            vmem((LANES, channels), BF16),
            vmem((images, LANES), F32),
            vmem((GROUP, images, LANES), F32),
            vmem((96, channels), BF16),
            vmem((wide4, channels), BF16),
            vmem((32, channels), F32),
            vmem((LANES, channels), jnp.int32),
            vmem((channels, channels), BF16),
            vmem((channels, wide5), BF16),
            vmem((pixels, wide4), BF16),
            vmem((pixels, wide5), BF16),
            vmem((tiles, H, W, LANES), F32),
            vmem((H + 4, W, LANES), F32),
            vmem((tiles, H, W, LANES), F32),
            vmem((H, W, LANES), BF16),
            vmem((H + 4, W, LANES), F32),
            vmem((pixels, channels), BF16),
            vmem((TAPS * TAPS, 8, LANES), F32),
            vmem((LANES, LANES), F32),
            vmem((pixels, wide4), BF16),
            vmem((tiles, SEGS, half, LANES), F32),
            vmem((tiles, SEGS, half, LANES), BF16),
            vmem((tiles, SEGS, half, LANES), BF16),
            vmem((GROUP, GROUP, half, LANES), BF16),
            vmem((GROUP, GROUP, half, LANES), BF16),
            vmem((Y, GROUP // 2, 16, LANES), BF16),
            vmem((Y, GROUP // 2, 16, LANES), BF16),
            vmem((Z, GROUP * KEEP, LANES), F32),
            vmem((2 * Z, GROUP * KEEP, LANES), F32),
            vmem((GROUP // X, GROUP * KEEP, LANES), F32),
            vmem((X, GROUP // X, GROUP * KEEP, LANES), F32),
            dma((2, CHUNKS)),
            dma((2, CHUNKS)),
            dma((GROUP,)),
            dma((GROUP,)),
            dma((GROUP,)),
            dma((GROUP,)),
            dma((tiles,)),
            dma((tiles,)),
            dma((GROUP, GROUP)),
            dma((GROUP, GROUP)),
            dma((2, Y)),
            dma((2, Y)),
            dma((Z, 2)),
            dma((2 * Z,)),
            dma((X,)),
            dma((X,)),
            dma((GROUP,)),
            dma((GROUP,)),
            dma(()),
        ],
        compiler_params=pltpu.CompilerParams(
            collective_id=0, has_side_effects=True, vmem_limit_bytes=56 * 1024 * 1024
        ),
        cost_estimate=pl.CostEstimate(
            flops=3_000_000_000, bytes_accessed=8_000_000, transcendentals=2_400_000
        ),
    )(*operands)
    grad_e, grad_d, grad_p, input_cotangent = pl.pallas_call(
        place_outputs,
        out_shape=(
            jax.ShapeDtypeStruct((tiles * KEEP, c4), F32),
            jax.ShapeDtypeStruct((tiles * KEEP, TAPS * TAPS), F32),
            jax.ShapeDtypeStruct((tiles * KEEP, c5), F32),
            jax.ShapeDtypeStruct((images, local_rows, W, c4), BF16),
        ),
        in_specs=[vm, vm],
        out_specs=(vm, vm, vm, vm),
    )(total, cots)
    return (grad_e.T, grad_d.T, grad_p, input_cotangent)


def solution(mesh):
    in_specs = (
        P("dp", "space", None, None),
        P(),
        P(),
        P(),
        P(),
        P(),
        P(),
        P(),
        P(("dp", "space"), None, None, None),
    )
    out_specs = (P(None, "dp"), P(None, "dp"), P("dp", None), P("dp", "space", None, None))
    return jax.shard_map(local, mesh=mesh, in_specs=in_specs, out_specs=out_specs, check_vma=False)
```

```python
import functools
import math

import jax
import jax.numpy as jnp
from jax import lax
from jax.experimental import pallas as pl
from jax.experimental.pallas import tpu as pltpu
from jax.sharding import PartitionSpec as P

H, W, LANES, RB = 32, 16, 128, 4
TAPS = 5
Y, Z, CORES, KEEP = 8, 4, 2, 2
GROUP = 8
X = 4
ORDER = (2, 6, 4, 1, 7, 3, 5, 0)
CHUNKS = 4
SEGS = 7
DW_AT = 88
F32, BF16 = jnp.float32, jnp.bfloat16
MESH = pl.DeviceIdType.MESH
ACROSS = (((1,), (1,)), ((), ()))


def sigmoid(value):
    return 0.5 * jnp.tanh(0.5 * value) + 0.5


def shifted(block, step):
    if step == 0:
        return block
    low, high = block[:, :8], block[:, 8:]
    at = lax.broadcasted_iota(jnp.int32, low.shape, 1)
    low_r = pltpu.roll(low, (-step) % 8, 1)
    high_r = pltpu.roll(high, (-step) % 8, 1)
    if step > 0:
        inside = at < 8 - step
        return jnp.concatenate(
            [jnp.where(inside, low_r, high_r), jnp.where(inside, high_r, 0.0)], axis=1
        )
    inside = at >= -step
    return jnp.concatenate(
        [jnp.where(inside, low_r, 0.0), jnp.where(inside, high_r, low_r)], axis=1
    )


def tile_forward(taps, spread, back_hidden, hidden, back_deep):
    def rows(at, carry):
        r = at * RB
        window = spread[pl.ds(r, RB + 4)]
        total = None
        for j in range(TAPS):
            part = None
            for i in range(TAPS):
                term = window[i : i + RB] * taps[i * TAPS + j]
                part = term if part is None else part + term
            part = shifted(part, j - 2)
            total = part if total is None else total + part
        sig = sigmoid(total)
        swish = total * sig
        hidden[pl.ds(r, RB)] = swish.astype(BF16)
        slope = sig + swish * (1.0 - sig)
        back_deep[pl.ds(r + 2, RB)] = back_hidden[pl.ds(r, RB)] * slope
        return carry

    lax.fori_loop(0, H // RB, rows, 0, unroll=True)


def tile_backward(taps, spread, back_deep, pre, back_pre, grad_taps):
    grad_taps[...] = jnp.zeros_like(grad_taps)

    def rows(at, carry):
        r = at * RB
        window = back_deep[pl.ds(r, RB + 4)]
        mine = spread[pl.ds(r + 2, RB)]
        total = None
        for j in range(TAPS):
            moved = shifted(mine, j - 2)
            part = None
            for i in range(TAPS):
                rows_i = window[TAPS - 1 - i : TAPS - 1 - i + RB]
                term = rows_i * taps[i * TAPS + j]
                part = term if part is None else part + term
                prod = rows_i * moved
                prod = prod[:, :8] + prod[:, 8:]
                prod = (prod[0] + prod[1]) + (prod[2] + prod[3])
                grad_taps[i * TAPS + j] += prod
            part = shifted(part, 2 - j)
            total = part if total is None else total + part
        value = pre[pl.ds(r, RB)]
        sig = sigmoid(value)
        slope = sig + value * sig * (1.0 - sig)
        back_pre[pl.ds(r * W, RB * W)] = (total * slope).astype(BF16).reshape(RB * W, LANES)
        return carry

    lax.fori_loop(0, H // RB, rows, 0, unroll=True)


def exchange(source, landed, send, recv, device):
    copy = pltpu.make_async_remote_copy(
        src_ref=source,
        dst_ref=landed,
        send_sem=send,
        recv_sem=recv,
        device_id=device,
        device_id_type=MESH,
    )
    copy.start()
    return copy


def arrived(source, landed, send, recv, device):
    pltpu.make_async_remote_copy(
        src_ref=source,
        dst_ref=landed,
        send_sem=send,
        recv_sem=recv,
        device_id=device,
        device_id_type=MESH,
    ).wait_recv()


def four_rows(x, taps, first, count):
    total = None
    for j in range(3):
        part = None
        for i in range(3):
            term = x[first + i : first + i + count] * taps[3 * i + j]
            part = term if part is None else part + term
        part = shifted(part, j - 1)
        total = part if total is None else total + part
    return total


def one_row(x, taps, i):
    total = None
    for j in range(3):
        part = shifted(x * taps[3 * i + j], j - 1)
        total = part if total is None else total + part
    return total


def kernel(
    scale, x_hbm, dw4_hbm, down_hbm, up_hbm, p4_hbm, e5_hbm, dw5_hbm, p5_hbm, cot_hbm, out_ref, cots_ref,
    x_ref, dw4_ref, down_ref, up_ref, p4_ref, e5_ref, dw5_ref, p5_ref, cot_ref, fetch,
    low, high, mixed, acc, gates, hid4, rows4, down, up, part, got_part, dw_split, exp_ref, dw_ref, offset, places, proj_ref,
    s_pad, cot_pad, pre, spread, bhid, hid, bdeep, bpre, gtaps, gsq, back,
    mine, give, got_core, sums, got_space, send_y, got_y, send_z, got_z, pick, got_x,
    halo_s, halo_r, part_s, part_r, sec_s, sec_r,
    core_s, core_r, space_s, space_r, y_s, y_r, z_s, z_r, all_s, all_r, cot_s, cot_r, local_sem,
):
    dp, sp = lax.axis_index("dp"), lax.axis_index("space")
    core = lax.rem(dp, CORES)
    z = lax.rem(lax.div(dp, CORES), Z)
    y = lax.div(dp, CORES * Z)
    other = 1 - core
    half = LANES // CORES

    def at_space(place):
        return (dp, place)

    def at_line(place):
        return (dp + (place[0] - z) * CORES, place[1] * X + x)

    def at_x(place):
        return (dp, z_lo * X + place)

    def at_y(place):
        return (dp + (place - y) * (CORES * Z), sp)

    sibling = (dp + other - core, sp)
    spaces = [lax.rem(sp + step, GROUP) for step in range(1, GROUP)]
    ys = [lax.rem(y + step, Y) for step in range(1, Y)]
    zs = [lax.rem(z + step, Z) for step in range(1, Z)]
    x, z_lo = lax.rem(sp, X), lax.div(sp, X)
    xs = [lax.rem(x + step, X) for step in range(1, X)]
    line = [(z, 1 - z_lo)] + [(p, e) for p in zs for e in range(GROUP // X)]

    barrier = pltpu.get_barrier_semaphore()
    everyone = [at_space(p) for p in spaces] + [sibling] + [at_y(p) for p in ys] + [at_line(p) for p in line[1:]]
    for device in everyone:
        pl.semaphore_signal(barrier, inc=1, device_id=device, device_id_type=MESH)

    def fetched(k, source, target):
        copy = pltpu.make_async_copy(source, target, fetch.at[k])
        copy.start()
        return copy

    x_in = fetched(0, x_hbm, x_ref)
    dw4_in = fetched(1, dw4_hbm, dw4_ref)
    e5_in = fetched(2, e5_hbm, e5_ref)
    dw5_in = fetched(3, dw5_hbm, dw5_ref)
    p5_in = fetched(4, p5_hbm, p5_ref)
    down_in = fetched(5, down_hbm, down_ref)
    up_in = fetched(6, up_hbm, up_ref)
    p4_in = fetched(7, p4_hbm, p4_ref)
    cot_in = fetched(8, cot_hbm, cot_ref)

    images, local_rows = x_ref.shape[:2]
    channels = x_ref.shape[3]
    chunk = images // CHUNKS
    cells = local_rows * W

    @pl.when(sp == 0)
    def _():
        low[...] = jnp.zeros_like(low)

    @pl.when(sp == GROUP - 1)
    def _():
        high[...] = jnp.zeros_like(high)

    pl.semaphore_wait(barrier, len(everyone))

    def down_copy(c):
        part = pl.ds(c * chunk, chunk)
        return pltpu.make_async_remote_copy(
            src_ref=x_hbm.at[part, local_rows - 1], dst_ref=low.at[part], send_sem=halo_s.at[0, c],
            recv_sem=halo_r.at[0, c], device_id=(dp, lax.rem(sp + 1, GROUP)), device_id_type=MESH,
        )

    def up_copy(c):
        part = pl.ds(c * chunk, chunk)
        return pltpu.make_async_remote_copy(
            src_ref=x_hbm.at[part, 0], dst_ref=high.at[part], send_sem=halo_s.at[1, c],
            recv_sem=halo_r.at[1, c], device_id=(dp, lax.rem(sp + GROUP - 1, GROUP)), device_id_type=MESH,
        )

    @pl.when(sp < GROUP - 1)
    def _():
        for c in range(CHUNKS):
            down_copy(c).start()

    @pl.when(sp > 0)
    def _():
        for c in range(CHUNKS):
            up_copy(c).start()

    x_in.wait()
    dw4_in.wait()

    def taps4(t):
        at = slice(t * LANES, (t + 1) * LANES)
        return [dw4_ref[k : k + 1, at].reshape(1, 1, LANES) for k in range(9)]

    def swish_rows(value):
        return value * sigmoid(value)

    def folded(rows):
        rows = rows[:, :8] + rows[:, 8:]
        return rows[0] + rows[1]

    def inner(n, carry):
        for t in range(channels // LANES):
            at = slice(t * LANES, (t + 1) * LANES)
            taps = taps4(t)
            x = x_ref[n, :, :, at].astype(F32)
            none = jnp.zeros((1, W, LANES), F32)
            value = four_rows(jnp.concatenate([none, x, none], axis=0), taps, 0, local_rows)
            done = swish_rows(value[1:3])
            mixed[n, 0:1, :, at] = value[0:1]
            mixed[n, 1:3, :, at] = done
            mixed[n, 3:4, :, at] = value[3:4]
            acc[n, :, at] = folded(done)
        return carry

    lax.fori_loop(0, images, inner, 0)

    e5_in.wait()
    dw5_in.wait()
    down_in.wait()
    up_in.wait()
    cot_in.wait()
    down[...] = jnp.zeros_like(down)
    down[: down_ref.shape[0]] = down_ref[...]
    up[...] = jnp.zeros_like(up)
    up[: up_ref.shape[0]] = up_ref[...]
    rows4[...] = jnp.zeros_like(rows4)
    cot_pad[...] = jnp.zeros_like(cot_pad)
    cot_pad[:, : cot_ref.shape[1]] = cot_ref[...]
    exp_ref[...] = jnp.zeros_like(exp_ref)
    proj_ref[...] = jnp.zeros_like(proj_ref)
    spread[...] = jnp.zeros_like(spread)
    bdeep[...] = jnp.zeros_like(bdeep)
    gsq[...] = jnp.zeros_like(gsq)
    sums[GROUP - 1, GROUP - 1] = jnp.zeros((half, LANES), BF16)
    dw_split[...] = jnp.zeros_like(dw_split)
    rest = dw5_ref[...]
    for k in range(3):
        top = rest.astype(BF16)
        dw_split[32 * k : 32 * k + TAPS * TAPS] = top
        rest = rest - top.astype(F32)
    tiles = channels // LANES
    each = channels // (Y * Z * CORES)

    at = lax.broadcasted_iota(jnp.int32, (LANES, channels), 0)
    shard = ((at >> 3) & 7) * (Z * CORES) + ((at >> 1) & 3) * CORES + (at >> 6)
    offset[...] = lax.broadcasted_iota(jnp.int32, (LANES, channels), 1) - shard * each - (at & 1)

    def reorder_expand(t, carry):
        lanes = pl.ds(pl.multiple_of(t * LANES, LANES), LANES)
        place = jnp.where(offset[...] == t * KEEP, 1.0, 0.0).astype(BF16)
        places[lanes] = place
        exp = lax.dot_general(e5_ref[...], place, ACROSS, preferred_element_type=F32)
        exp_ref[: e5_ref.shape[0], lanes] = exp.astype(BF16)
        taps = lax.dot_general(dw_split[...], place, ACROSS, preferred_element_type=F32)
        dw_ref[:, lanes] = taps[:32] + taps[32:64] + taps[64:]
        return carry

    lax.fori_loop(0, tiles, reorder_expand, 0)

    for c in range(CHUNKS):

        @pl.when(sp > 0)
        def _():
            down_copy(c).wait_recv()

        @pl.when(sp < GROUP - 1)
        def _():
            up_copy(c).wait_recv()

        def outer(n, carry):
            for t in range(tiles):
                at = slice(t * LANES, (t + 1) * LANES)
                taps = taps4(t)
                above = low[n, :, at].astype(F32).reshape(1, W, LANES)
                below = high[n, :, at].astype(F32).reshape(1, W, LANES)
                first = swish_rows(mixed[n, 0:1, :, at] + one_row(above, taps, 0))
                last = swish_rows(mixed[n, 3:4, :, at] + one_row(below, taps, 2))
                mixed[n, 0:1, :, at] = first
                mixed[n, 3:4, :, at] = last
                acc[n, :, at] += folded(jnp.concatenate([first, last], axis=0))
            return carry

        lax.fori_loop(c * chunk, (c + 1) * chunk, outer, 0)

    mean = jnp.sum(acc[...], axis=1) / (GROUP * cells)
    top = mean.astype(BF16)
    rest = (mean - top.astype(F32)).astype(BF16)
    value = lax.dot_general(top, down[...], ACROSS, preferred_element_type=F32)
    value += lax.dot_general(rest, down[...], ACROSS, preferred_element_type=F32)
    part[...] = value
    sent = [exchange(part, got_part.at[sp], part_s.at[p], part_r.at[sp], at_space(p)) for p in spaces]
    p5_in.wait()

    def reorder_project(h):
        at = slice(h * channels // 3, (h + 1) * channels // 3)
        proj = lax.dot_general(places[at], p5_ref[...], ACROSS, preferred_element_type=F32)
        proj_ref[at, : p5_ref.shape[0]] = proj.astype(BF16)

    reorder_project(0)
    reorder_project(1)
    for p in spaces:
        arrived(part, got_part.at[p], part_s.at[p], part_r.at[p], at_space(p))
    for p in spaces:
        value += got_part[p]
    squeezed = swish_rows(value).astype(BF16)
    gates[...] = sigmoid(jnp.dot(squeezed, up[...], preferred_element_type=F32))

    order = [lax.rem(sp + step, GROUP) for step in ORDER]
    def rows4_of(k):
        return rows4.at[k * cells : (k + 1) * cells]

    def landing(place):
        return s_pad.at[pl.ds(pl.multiple_of(place * cells, cells), cells)]

    p4_in.wait()
    part_rows = images * cells // 2
    for h in range(2):
        for k in range(h * images // 2, (h + 1) * images // 2):
            n = order[k]
            gated = mixed[n].reshape(cells, channels) * gates[pl.ds(n, 1)]
            hid4[k * cells : (k + 1) * cells] = gated.astype(BF16)
        at = slice(h * part_rows, (h + 1) * part_rows)
        value = lax.dot_general(hid4[at], p4_ref[...], ACROSS, preferred_element_type=F32)
        rows4[at, : p4_ref.shape[0]] = value.astype(BF16)
        for k in range(h * images // 2, min((h + 1) * images // 2, images - 1)):
            n = order[k]
            exchange(rows4_of(k), landing(sp), sec_s.at[n], sec_r.at[sp], at_space(n))

    mine_at = pl.ds(pl.multiple_of(sp * cells, cells), cells)
    s_pad[mine_at] = rows4[(images - 1) * cells :]

    reorder_project(2)

    def back_hidden(t, carry):
        lanes = pl.ds(pl.multiple_of(t * LANES, LANES), LANES)
        bh = lax.dot_general(
            cot_pad[...], proj_ref[lanes], ACROSS, preferred_element_type=F32
        )
        bhid[t] = bh.reshape(H, W, LANES)
        return carry

    lax.fori_loop(0, tiles, back_hidden, 0)
    for p in spaces:
        arrived(rows4_of(0), landing(p), sec_s.at[p], sec_r.at[p], at_space(p))

    for h in range(3):
        wide = channels // 3
        value = jnp.dot(s_pad[...], exp_ref[:, h * wide : (h + 1) * wide], preferred_element_type=F32)
        for t in range(tiles // 3):
            pre[h * (tiles // 3) + t] = value[:, t * LANES : (t + 1) * LANES].reshape(H, W, LANES)

    def put(t, q, block):
        low, high = block[:half], block[half:]
        mine[t, q] = jnp.where(core == 0, low, high)
        give[t, q] = jnp.where(core == 0, high, low).astype(BF16)

    def send_block(owner, slot):
        @pl.when(owner != sp)
        def _():
            exchange(
                sums.at[owner, slot], got_space.at[sp, slot], space_s.at[owner, slot],
                space_r.at[sp, slot], at_space(owner),
            )

    def finish(t):
        arrived(give.at[t], got_core.at[t], core_s.at[t], core_r.at[t], sibling)
        for step in range(SEGS):
            q = lax.rem(sp + step, SEGS)
            b = t * SEGS + q
            owner, slot = lax.rem(b, GROUP), lax.div(b, GROUP)
            sums[owner, slot] = (mine[t, q] + got_core[t, q].astype(F32)).astype(BF16)
            send_block(owner, slot)

    def tile(t, carry):
        lanes = pl.ds(pl.multiple_of(t * LANES, LANES), LANES)
        pre_v = pre[t]
        spread[2 : 2 + H] = (pre_v * sigmoid(pre_v)).astype(BF16).astype(F32)
        taps = [dw_ref[k : k + 1, lanes].reshape(1, 1, LANES) for k in range(TAPS * TAPS)]
        tile_forward(taps, spread, bhid.at[t], hid, bdeep)
        gp = lax.dot_general(
            hid[...].reshape(H * W, LANES), cot_pad[...], (((0,), (0,)), ((), ())),
            preferred_element_type=F32,
        )
        for q in range(4):
            put(t, q, gp[:, q * LANES : (q + 1) * LANES])
        tile_backward(taps, spread, bdeep, pre.at[t], bpre.at[:, lanes], gtaps)
        bp = bpre[:, lanes]
        ge = lax.dot_general(
            bp, s_pad[...], (((0,), (0,)), ((), ())), preferred_element_type=F32
        )
        gsq[DW_AT : DW_AT + TAPS * TAPS] = jnp.sum(gtaps[...], axis=1)
        put(t, 4, ge[:, :LANES])
        put(t, 5, ge[:, LANES : 2 * LANES])
        put(t, 6, ge[:, 2 * LANES :] + gsq[...].T)
        exchange(give.at[t], got_core.at[t], core_s.at[t], core_r.at[t], sibling)

        @pl.when(t > 0)
        def _():
            finish(t - 1)

        return carry

    lax.fori_loop(0, tiles, tile, 0)
    parts = ((0, GROUP // 2 - 1), (GROUP // 2 - 1, GROUP // 2))

    def gathered(first, last):
        for b in range(first, last):
            pair = []
            for slot in (2 * b, 2 * b + 1):
                for p in spaces:
                    arrived(
                        sums.at[p, slot], got_space.at[p, slot], space_s.at[p, slot],
                        space_r.at[p, slot], at_space(p),
                    )
                block = sums[sp, slot].astype(F32)
                for p in spaces:
                    block += got_space[p, slot].astype(F32)
                pair.append(block.reshape(Y, 8, LANES))
            send_y[:, b] = jnp.concatenate(pair, axis=1).astype(BF16)
        h = parts.index((first, last))
        for p in ys:
            sent.append(
                exchange(
                    send_y.at[p, first:last], got_y.at[y, first:last], y_s.at[h, p], y_r.at[h, y], at_y(p)
                )
            )

    gathered(*parts[0])
    finish(tiles - 1)
    send_block(GROUP - 1, GROUP - 1)
    back[...] = lax.dot_general(
        bpre[...], exp_ref[...], ACROSS, preferred_element_type=F32
    ).astype(BF16)

    rows = back.shape[0] // GROUP

    def rows_of(place):
        return back.at[pl.ds(pl.multiple_of(place * rows, rows), rows)]

    gathered(GROUP // 2 - 1, GROUP // 2)
    sent += [
        exchange(rows_of(p), cots_ref.at[sp], cot_s.at[p], cot_r.at[sp], at_space(p))
        for p in spaces
    ]
    own = pltpu.make_async_copy(rows_of(sp), cots_ref.at[sp], local_sem)
    own.start()

    summed = []
    for h, (first, last) in enumerate(parts):
        for p in ys:
            arrived(send_y.at[p, first:last], got_y.at[p, first:last], y_s.at[h, p], y_r.at[h, p], at_y(p))
        value = send_y[y, first:last].astype(F32)
        for p in ys:
            value += got_y[p, first:last].astype(F32)
        summed.append(value)
    summed = (jnp.concatenate(summed, axis=0) * scale).reshape(GROUP, 8, LANES)

    for p in range(Z):
        for b in range(GROUP):
            send_z[p, KEEP * b : KEEP * (b + 1)] = summed[b, KEEP * p : KEEP * (p + 1)]
    me = z * 2 + z_lo
    sent += [
        exchange(send_z.at[p], got_z.at[me], z_s.at[p, e], z_r.at[me], at_line((p, e))) for p, e in line
    ]
    got_z[me] = send_z[z]
    for p, e in line:
        arrived(send_z.at[p], got_z.at[p * 2 + e], z_s.at[p, e], z_r.at[p * 2 + e], at_line((p, e)))
    for e in range(GROUP // X):
        value = got_z[e]
        for p in range(1, Z):
            value += got_z[p * 2 + e]
        pick[e] = value

    got_x[x] = pick[...]
    sent += [exchange(pick, got_x.at[x], all_s.at[p], all_r.at[x], at_x(p)) for p in xs]
    for p in xs:
        arrived(pick, got_x.at[p], all_s.at[p], all_r.at[p], at_x(p))
    for b in range(tiles * SEGS):
        t, q = divmod(b, SEGS)
        slot, owner = divmod(b, GROUP)
        out_ref[KEEP * t : KEEP * (t + 1), q * LANES : (q + 1) * LANES] = got_x[
            owner % X, owner // X, KEEP * slot : KEEP * (slot + 1)
        ]
    for p in spaces:
        arrived(rows_of(p), cots_ref.at[p], cot_s.at[p], cot_r.at[p], at_space(p))
    own.wait()
    for copy in sent:
        copy.wait_send()

    def drain_core(t, carry):
        pltpu.make_async_remote_copy(
            src_ref=give.at[t], dst_ref=got_core.at[t], send_sem=core_s.at[t],
            recv_sem=core_r.at[t], device_id=sibling, device_id_type=MESH,
        ).wait_send()
        return carry

    lax.fori_loop(0, tiles, drain_core, 0)

    def drain_space(slot, carry):
        for p in spaces:
            pltpu.make_async_remote_copy(
                src_ref=sums.at[p, slot], dst_ref=got_space.at[sp, slot],
                send_sem=space_s.at[p, slot], recv_sem=space_r.at[sp, slot],
                device_id=at_space(p), device_id_type=MESH,
            ).wait_send()
        return carry

    lax.fori_loop(0, GROUP, drain_space, 0)
    for p in spaces:
        pltpu.make_async_remote_copy(
            src_ref=rows4_of(0), dst_ref=landing(sp), send_sem=sec_s.at[p], recv_sem=sec_r.at[sp],
            device_id=at_space(p), device_id_type=MESH,
        ).wait_send()

    @pl.when(sp < GROUP - 1)
    def _():
        for c in range(CHUNKS):
            down_copy(c).wait_send()

    @pl.when(sp > 0)
    def _():
        for c in range(CHUNKS):
            up_copy(c).wait_send()


def place_outputs(total, cots, grad_e, grad_d, grad_p, input_cotangent):
    grad_p[...] = total[:, : grad_p.shape[1]]
    grad_e[...] = total[:, 4 * LANES : 4 * LANES + grad_e.shape[1]]
    grad_d[...] = total[:, 6 * LANES :][:, DW_AT : DW_AT + TAPS * TAPS]
    input_cotangent[...] = cots[:, :, : input_cotangent.shape[3]].reshape(input_cotangent.shape)


def local(
    expanded,
    dw_four,
    squeeze_down,
    squeeze_up,
    project_four,
    expand_five,
    dw_five,
    project_five,
    cotangent,
):
    images, local_rows, _, channels = expanded.shape
    c4, c5 = expand_five.shape[0], cotangent.shape[3]
    pixels, wide4, wide5 = H * W, 3 * LANES, 4 * LANES
    tiles, half = channels // LANES, LANES // CORES
    total_pixels = images * lax.axis_size("dp") * pixels
    vm = pl.BlockSpec(memory_space=pltpu.VMEM)
    dma = pltpu.SemaphoreType.DMA
    vmem = pltpu.VMEM
    operands = (
        expanded, dw_four, squeeze_down.T, squeeze_up, project_four.T, expand_five, dw_five, project_five.T,
        cotangent.reshape(pixels, c5),
    )
    total, cots = pl.pallas_call(
        functools.partial(kernel, 1.0 / math.sqrt(total_pixels)),
        out_shape=(
            jax.ShapeDtypeStruct((tiles * KEEP, SEGS * LANES), F32),
            jax.ShapeDtypeStruct((GROUP, pixels // GROUP, wide4), BF16),
        ),
        in_specs=[pl.BlockSpec(memory_space=pl.ANY)] * 9,
        out_specs=(vm, vm),
        scratch_shapes=[
            *[vmem(a.shape, a.dtype) for a in operands],
            dma((len(operands),)),
            vmem((images, W, channels), BF16),
            vmem((images, W, channels), BF16),
            vmem(expanded.shape, F32),
            vmem((images, 8, channels), F32),
            vmem((images, channels), F32),
            vmem((pixels, channels), BF16),
            vmem((pixels, wide4), BF16),
            vmem((LANES, channels), BF16),
            vmem((LANES, channels), BF16),
            vmem((images, LANES), F32),
            vmem((GROUP, images, LANES), F32),
            vmem((96, channels), BF16),
            vmem((wide4, channels), BF16),
            vmem((32, channels), F32),
            vmem((LANES, channels), jnp.int32),
            vmem((channels, channels), BF16),
            vmem((channels, wide5), BF16),
            vmem((pixels, wide4), BF16),
            vmem((pixels, wide5), BF16),
            vmem((tiles, H, W, LANES), F32),
            vmem((H + 4, W, LANES), F32),
            vmem((tiles, H, W, LANES), F32),
            vmem((H, W, LANES), BF16),
            vmem((H + 4, W, LANES), F32),
            vmem((pixels, channels), BF16),
            vmem((TAPS * TAPS, 8, LANES), F32),
            vmem((LANES, LANES), F32),
            vmem((pixels, wide4), BF16),
            vmem((tiles, SEGS, half, LANES), F32),
            vmem((tiles, SEGS, half, LANES), BF16),
            vmem((tiles, SEGS, half, LANES), BF16),
            vmem((GROUP, GROUP, half, LANES), BF16),
            vmem((GROUP, GROUP, half, LANES), BF16),
            vmem((Y, GROUP // 2, 16, LANES), BF16),
            vmem((Y, GROUP // 2, 16, LANES), BF16),
            vmem((Z, GROUP * KEEP, LANES), F32),
            vmem((2 * Z, GROUP * KEEP, LANES), F32),
            vmem((GROUP // X, GROUP * KEEP, LANES), F32),
            vmem((X, GROUP // X, GROUP * KEEP, LANES), F32),
            dma((2, CHUNKS)),
            dma((2, CHUNKS)),
            dma((GROUP,)),
            dma((GROUP,)),
            dma((GROUP,)),
            dma((GROUP,)),
            dma((tiles,)),
            dma((tiles,)),
            dma((GROUP, GROUP)),
            dma((GROUP, GROUP)),
            dma((2, Y)),
            dma((2, Y)),
            dma((Z, 2)),
            dma((2 * Z,)),
            dma((X,)),
            dma((X,)),
            dma((GROUP,)),
            dma((GROUP,)),
            dma(()),
        ],
        compiler_params=pltpu.CompilerParams(
            collective_id=0, has_side_effects=True, vmem_limit_bytes=56 * 1024 * 1024
        ),
        cost_estimate=pl.CostEstimate(
            flops=3_000_000_000, bytes_accessed=8_000_000, transcendentals=2_400_000
        ),
    )(*operands)
    grad_e, grad_d, grad_p, input_cotangent = pl.pallas_call(
        place_outputs,
        out_shape=(
            jax.ShapeDtypeStruct((tiles * KEEP, c4), F32),
            jax.ShapeDtypeStruct((tiles * KEEP, TAPS * TAPS), F32),
            jax.ShapeDtypeStruct((tiles * KEEP, c5), F32),
            jax.ShapeDtypeStruct((images, local_rows, W, c4), BF16),
        ),
        in_specs=[vm, vm],
        out_specs=(vm, vm, vm, vm),
    )(total, cots)
    return (grad_e.T, grad_d.T, grad_p, input_cotangent)


def solution(mesh):
    in_specs = (
        P("dp", "space", None, None),
        P(),
        P(),
        P(),
        P(),
        P(),
        P(),
        P(),
        P(("dp", "space"), None, None, None),
    )
    out_specs = (P(None, "dp"), P(None, "dp"), P("dp", None), P("dp", "space", None, None))
    return jax.shard_map(local, mesh=mesh, in_specs=in_specs, out_specs=out_specs, check_vma=False)
```
